32 devices in a mesh: shard: 4 (over z), group: 8 (over y, x, core).
Axes of the slice: x: 2, y: 2, z: 4, core: 2. Of those that a mesh axis runs over, the one named last changes fastest.
Arguments:
- item_ids: int32 [4096], P(('shard', 'group')), may hold values from 0 to 1023, as said below
- seq_lengths: int32 [32, 8], P(('shard', 'group')), may hold values from 1 to 64, 128 in all within a row
- time_buckets: int32 [4096], P(('shard', 'group')), may hold values from 0 to 63
- neg_ids: int32 [4, 256], P('shard', 'group'), may hold values from 0 to 1023, as said below
- table: float32 [1024, 512], P('group'), may hold values from -6 to 6
- w_in: float32 [512, 2048], replicated, may hold values from -0.25 to 0.25
- b_in: float32 [2048], replicated, may hold values from -3 to 3
- w_out: float32 [512, 512], replicated, may hold values from -0.25 to 0.25
- rab: float32 [4, 64], replicated, may hold values from -4 to 4
Outputs:
- table_grad: float32 [1024, 512], P('group')
- token_loss: float32 [4096], P(('shard', 'group'))
The draws below stay inside these ranges and needn't reach their ends.
Inputs may be any that keep to these rules, and one draw needn't show every extreme that they name: `item_ids`: item i is held by the rows of group index i // 128. The 128 tokens of one device name items of any one group index at most 32 times; in every draw, for each shard index, one group index is named exactly 32 times by every device of that shard index. `neg_ids`: entry r of a row names an item of group index r // 32.
All inputs are finite; a program needn't handle non-finite values.
Results may differ from the reference program's by a relative error of at most 0.0003.
Values sent between devices are 32-bit elements; how exact they have to be, the bound alone decides.
No kernel may reach another device: no remote copies, remote signals or barrier semaphores. Data moves between devices by JAX's collectives and lax.ppermute only.
A program may use at most 64 MiB of HBM per device.

```python
import math
import jax
import jax.numpy as jnp
import numpy as np
from jax import lax

D = 512
HEADS = 4
NB = 64
TOK_DEV = 128
SEQ_DEV = 8
MOST_LEN = 64
ROWS_DEV = 128
NEG_DEV = 32
NEG = 256
CAP = 32
ITEMS = 1024
TOKENS = 4096
N_SHARD = 4
N_GROUP = 8


def draw_item_ids(key, part):
    slots = N_GROUP * CAP
    devices = N_SHARD * N_GROUP
    hot_key, dev_key = jax.random.split(jax.random.fold_in(key, 11))
    hot = jax.random.randint(hot_key, (N_SHARD,), 0, N_GROUP)

    def one(dkey, hot_owner):
        first, second, third = jax.random.split(dkey, 3)
        order = jax.random.permutation(first, slots)
        owners = order // CAP
        rank = jnp.argsort((owners != hot_owner).astype(jnp.int32), stable=True)
        chosen = jax.random.permutation(second, owners[rank][:TOK_DEV])
        rows = jax.random.randint(third, (TOK_DEV,), 0, ROWS_DEV)
        return chosen * ROWS_DEV + rows
    keys = jax.random.split(dev_key, devices)
    hots = jnp.repeat(hot, N_GROUP)
    return jax.vmap(one)(keys, hots).reshape(-1).astype(jnp.int32)


def draw_neg_ids(key, part):
    column = jnp.arange(NEG, dtype=jnp.int32)
    rows = jax.random.randint(jax.random.fold_in(key, 23), (N_SHARD, NEG), 0, ROWS_DEV)
    return ((column // NEG_DEV)[None, :] * ROWS_DEV + rows).astype(jnp.int32)


def touch_ends(result, key, low, top_value):
    longest = result.shape.index(max(result.shape))
    spots = []
    for shift in (0, 1):
        where = [jax.random.randint(jax.random.fold_in(key, axis), (), 0, length) for axis, length in enumerate(result.shape)]
        where[longest] = (where[longest] + shift) % result.shape[longest]
        spots.append(tuple(where))
    return result.at[spots[0]].set(low).at[spots[1]].set(top_value)


def level_of(own_key, shape, shards, least, high):
    loudness = 1.0
    for dim, parts in shards:
        heights = jax.random.uniform(jax.random.fold_in(jax.random.fold_in(own_key, 6), dim), (parts,), jnp.float32, least / len(shards), high / len(shards))
        loudness = loudness * jnp.repeat(jnp.exp(heights), shape[dim] // parts).reshape((-1,) + (1,) * (len(shape) - 1 - dim))
    return loudness


def split_up(amount, total, most, slope):
    weights = [(1 << 20) // math.isqrt(standing ** slope) + 1 for standing in range(2, amount + 1)]
    rest, holding = total - most - (amount - 1), [1] * (amount - 1)
    while rest > 0:
        free = [i for i in range(amount - 1) if holding[i] < most]
        pool, remaining = sum([weights[i] for i in free]), rest
        for i in free:
            extra = min(most - holding[i], max(1, remaining * weights[i] // pool), rest)
            holding[i] = holding[i] + extra
            rest = rest - extra
    return np.array([most] + holding)


def ragged_sizes(rng, number_of, total, limit, lean):
    if number_of == 2:
        one = jax.random.randint(rng, (), max(1, total - limit), min(limit, total - 1) + 1)
        return jnp.stack([one, total - one])
    tallies = jnp.asarray(split_up(number_of, total, limit, lean), jnp.int32)
    twos = (number_of - 1) // 2
    donor, taker = tallies[1:1 + 2 * twos:2], tallies[2:2 + 2 * twos:2]
    room = jnp.minimum(donor - 1, limit - taker)
    shifted = jax.random.randint(jax.random.fold_in(rng, 1), (twos,), 0, 1 << 20) % (room + 1)
    tallies = tallies.at[1:1 + 2 * twos:2].set(donor - shifted).at[2:2 + 2 * twos:2].set(taker + shifted)
    return tallies[jax.random.permutation(jax.random.fold_in(rng, 2), number_of)]


def gaussian(key, shape, scale, reach, cuts=(), kind=jnp.bfloat16):
    level = level_of(key, shape, cuts, -0.22, 0.18) if cuts else 1.0
    array = jax.random.normal(key, shape, jnp.float32) * scale * level
    return jnp.minimum(jnp.maximum(array, -reach), reach).astype(kind)


def setup_inputs(seed: int = 0) -> dict:
    key_of = jax.random.split(jax.random.key(seed), 10)
    item_ids = draw_item_ids(jax.random.fold_in(key_of[9], 71), 0)
    seq_lengths = jax.vmap(lambda own: ragged_sizes(own, SEQ_DEV, TOK_DEV, MOST_LEN, 2))(jax.random.split(key_of[1], (N_SHARD * N_GROUP))).reshape((N_SHARD * N_GROUP, SEQ_DEV)).astype(jnp.int32)
    time_buckets = touch_ends(jax.random.randint(key_of[2], (TOKENS,), 0, NB), jax.random.fold_in(key_of[2], 1), 0, NB - 1).astype(jnp.int32)
    neg_ids = draw_neg_ids(jax.random.fold_in(key_of[9], 71), 0)
    table = gaussian(key_of[4], (ITEMS, D), 1.0, 6.0, ((0, 8),), jnp.float32)
    w_in = gaussian(key_of[5], (D, 4 * D), D ** -0.5, 0.25, (), jnp.float32)
    b_in = gaussian(key_of[6], (4 * D,), 0.5, 3.0, (), jnp.float32)
    w_out = gaussian(key_of[7], (D, D), D ** -0.5, 0.25, (), jnp.float32)
    rab = gaussian(key_of[8], (HEADS, NB), 1.0, 4.0, (), jnp.float32)
    return dict(item_ids=item_ids, seq_lengths=seq_lengths, time_buckets=time_buckets, neg_ids=neg_ids, table=table, w_in=w_in, b_in=b_in, w_out=w_out, rab=rab)


HIGH = lax.Precision.HIGHEST
TEMPER = 0.05

def layer_norm(value):
    mean = lax.optimization_barrier(jnp.mean(value, -1, keepdims=True))
    centered = value - mean
    var = lax.optimization_barrier(jnp.mean(centered * centered, -1, keepdims=True))
    return centered * lax.rsqrt(var + 1e-05)

def unit(value):
    return value * lax.rsqrt(lax.optimization_barrier(jnp.sum(value * value, -1, keepdims=True)) + 1e-06)

def time_bias(buckets, rab, dtype):
    nbuck = rab.shape[1]
    levels = jnp.arange(nbuck, dtype=jnp.int32)
    gapgrid = jnp.abs(levels[:, None] - levels[None, :])
    gap_hot = (gapgrid[:, :, None] == levels[None, None, :]).astype(dtype)
    pair_bias = jnp.einsum('nmd,hd->hnm', gap_hot, rab, precision=HIGH)
    token_hot = (buckets[:, None] == levels[None, :]).astype(dtype)
    left = jnp.einsum('in,hnm->him', token_hot, pair_bias, precision=HIGH)
    return jnp.einsum('him,jm->hij', left, token_hot, precision=HIGH)

def hstu(emb, buckets, segment, w_in, b_in, w_out, rab):
    count = emb.shape[0]
    heads = rab.shape[0]
    hidden = jax.nn.silu(jnp.dot(layer_norm(emb), w_in, precision=HIGH, preferred_element_type=jnp.float32) + b_in)
    upart, vpart, qpart, kpart = jnp.split(hidden, 4, axis=1)
    qpart = qpart.reshape(count, heads, -1)
    kpart = kpart.reshape(count, heads, -1)
    vpart = vpart.reshape(count, heads, -1)
    scores = jnp.einsum('ihd,jhd->hij', qpart, kpart, precision=HIGH) * qpart.shape[2] ** (-0.5)
    scores = scores + time_bias(buckets, rab, emb.dtype)
    places = jnp.arange(count, dtype=jnp.int32)
    allowed = (places[None, :] <= places[:, None]) & (segment[None, :] == segment[:, None])
    weights = jax.nn.silu(scores) * allowed.astype(emb.dtype) / MOST_LEN
    mixed = jnp.einsum('hij,jhd->ihd', weights, vpart, precision=HIGH).reshape(count, -1)
    return jnp.dot(layer_norm(mixed) * upart, w_out, precision=HIGH, preferred_element_type=jnp.float32) + emb

def segments_of(lengths, count):
    ends = jnp.cumsum(lengths)
    places = jnp.arange(count, dtype=jnp.int32)
    segment = lax.optimization_barrier(jnp.sum((places[:, None] >= ends[None, :]).astype(jnp.int32), 1))
    following = jnp.concatenate([segment[1:], jnp.full((1,), -1, segment.dtype)])
    valid = (following == segment).astype(jnp.float32)
    return (segment, valid)

def device_terms(emb, buckets, lengths, negatives, w_in, b_in, w_out, rab):
    segment, valid = segments_of(lengths, emb.shape[0])
    valid = valid.astype(emb.dtype)

    def loss_of(inputs):
        states = unit(hstu(inputs, buckets, segment, w_in, b_in, w_out, rab))
        target = jnp.concatenate([inputs[1:], jnp.zeros((1, inputs.shape[1]), inputs.dtype)])
        target = unit(target)
        positive = lax.optimization_barrier(jnp.sum(states * target, -1)) / TEMPER
        logits = jnp.dot(states, negatives.T, precision=HIGH, preferred_element_type=jnp.float32) / TEMPER
        total = jnp.exp(positive) + lax.optimization_barrier(jnp.sum(jnp.exp(logits), 1))
        loss = valid * (jnp.log(total) - positive)
        return (jnp.sum(loss), loss)
    primal, back, loss = jax.vjp(loss_of, emb, has_aux=True)
    grad = back(jnp.ones((), emb.dtype))[0]
    return (grad, loss)

def reference(item_ids, seq_lengths, time_buckets, neg_ids, table, w_in, b_in, w_out, rab):
    width = table.shape[1]
    devices = N_SHARD * N_GROUP
    emb = table[item_ids].reshape(devices, TOK_DEV, width)
    buckets = time_buckets.reshape(devices, TOK_DEV)
    negatives = unit(table[neg_ids])

    def one(index):
        shard_index = index // N_GROUP
        return device_terms(emb[index], buckets[index], seq_lengths[index], negatives[shard_index], w_in, b_in, w_out, rab)
    grads, losses = lax.map(one, jnp.arange(devices, dtype=jnp.int32))
    table_grad = jax.ops.segment_sum(grads.reshape(-1, width), item_ids, num_segments=ROWS_DEV * N_GROUP)
    return (table_grad, losses.reshape(-1))
```

```python
import functools

import jax
import jax.numpy as jnp
from jax import lax
from jax.experimental import pallas as pl
from jax.experimental.pallas import tpu as pltpu
from jax.sharding import PartitionSpec as P

MOST_LEN = 64
TEMPER = 0.05
LANES = 128
F32 = jnp.float32
BF16 = jnp.bfloat16
NN = (((1,), (0,)), ((), ()))
NT = (((1,), (1,)), ((), ()))
TN = (((0,), (0,)), ((), ()))
VMEM = pl.BlockSpec(memory_space=pltpu.VMEM)
SMEM = pl.BlockSpec(memory_space=pltpu.SMEM)
PARAMS = pltpu.CompilerParams(vmem_limit_bytes=40 * 1024 * 1024)


def halves(value):
    high = value.astype(BF16)
    return high, (value - high.astype(F32)).astype(BF16)


def mul(left, right, dims=NN):
    lh, ll = left
    rh, rl = right
    dot = functools.partial(lax.dot_general, dimension_numbers=dims, preferred_element_type=F32)
    return dot(lh, rh) + (dot(ll, rh) + dot(lh, rl))


def pick(hot, value, dims=NN):
    high = value.astype(BF16)
    rest = value - high.astype(F32)
    mid = rest.astype(BF16)
    low = (rest - mid.astype(F32)).astype(BF16)
    dot = functools.partial(lax.dot_general, dimension_numbers=dims, preferred_element_type=F32)
    return dot(hot, high) + (dot(hot, mid) + dot(hot, low))


def sum_last(value):
    return jnp.sum(value, axis=-1, keepdims=True)


def mean_last(value):
    return jnp.mean(value, axis=-1, keepdims=True)


def lanes(shape):
    return lax.broadcasted_iota(jnp.int32, shape, 1)


def rows(shape):
    return lax.broadcasted_iota(jnp.int32, shape, 0)


def spread(row, count):
    wide = jnp.broadcast_to(row.astype(F32), (count, count))
    return wide.T.astype(jnp.int32)


def norm_of(value):
    centered = value - mean_last(value)
    scale = lax.rsqrt(mean_last(centered * centered) + 1e-05)
    return centered * scale, scale


def norm_back(grad, normed, scale):
    return scale * (grad - mean_last(grad) - normed * mean_last(grad * normed))


def unit_of(value):
    scale = lax.rsqrt(sum_last(value * value) + 1e-06)
    return value * scale, scale


def unit_back(grad, united, scale):
    return scale * (grad - united * sum_last(grad * united))


def prep_kernel(w_in, w_out, rab, buckets, in_h, in_l, out_h, out_l, bias):
    in_h[...], in_l[...] = halves(w_in[...])
    out_h[...], out_l[...] = halves(w_out[...])
    count = buckets.shape[1]
    mine = jnp.broadcast_to(buckets[...], (count, count))
    gap = jnp.abs(mine - spread(buckets[...], count))
    heads, nbuck = rab.shape
    for head in range(heads):
        level = jnp.concatenate([rab[head : head + 1, :], jnp.zeros((1, LANES - nbuck), F32)], 1)
        level = jnp.broadcast_to(level, (count, LANES))
        bias[head] = jnp.take_along_axis(level, gap, axis=1)


def prepare(w_in, w_out, rab, buckets):
    count = buckets.shape[0]
    width, hidden = w_in.shape
    heads = rab.shape[0]
    sds = jax.ShapeDtypeStruct
    return pl.pallas_call(
        prep_kernel,
        out_shape=(
            sds((width, hidden), BF16),
            sds((width, hidden), BF16),
            sds((width, width), BF16),
            sds((width, width), BF16),
            sds((heads, count, count), F32),
        ),
        in_specs=[VMEM] * 4,
        out_specs=(VMEM,) * 5,
        compiler_params=PARAMS,
        cost_estimate=pl.CostEstimate(flops=10_000_000, bytes_accessed=12_000_000, transcendentals=0),
        name="prepare",
    )(w_in, w_out, rab, buckets.reshape(1, count))


def layer_kernel(pieces, where, lengths, *refs):
    where = where[0]
    packed = refs[:pieces]
    in_h, in_l, b_in, out_h, out_l, bias = refs[pieces : pieces + 6]
    loss_ref = refs[pieces + 6]
    grads = refs[pieces + 7 : -1]
    whole = refs[-1]
    heads, count, _ = bias.shape
    width = in_h.shape[0]
    each = width // heads
    emb = packed[0][:count]
    for other in packed[1:]:
        emb = emb + other[:count]
    square = (count, count)
    seg_i = jnp.zeros(square, jnp.int32)
    seg_j = jnp.zeros(square, jnp.int32)
    seg_n = jnp.zeros((count, 1), jnp.int32)
    place_i, place_j, place = rows(square), lanes(square), rows((count, 1))
    end = jnp.int32(0)
    for index in range(lengths.shape[1]):
        end = end + lengths[0, index]
        seg_i = seg_i + (place_i >= end).astype(jnp.int32)
        seg_j = seg_j + (place_j >= end).astype(jnp.int32)
        seg_n = seg_n + (place + 1 >= end).astype(jnp.int32)
    allowed = jnp.where((place_j <= place_i) & (seg_i == seg_j), 1.0 / MOST_LEN, 0.0).astype(F32)
    valid = jnp.where((seg_n == seg_i[:, :1]) & (place + 1 < count), 1.0, 0.0).astype(F32)
    xn, x_scale = norm_of(emb)
    w_in = (in_h[...], in_l[...])
    w_out = (out_h[...], out_l[...])
    pre = mul(halves(xn), w_in) + b_in[...]
    sig = jax.nn.sigmoid(pre)
    hidden = pre * sig
    slope = sig * (1.0 + pre * (1.0 - sig))
    upart = hidden[:, :width]
    kept = []
    mixed = []
    for head in range(heads):
        vh, qh, kh = (
            halves(hidden[:, width * part + each * head : width * part + each * (head + 1)])
            for part in (1, 2, 3)
        )
        score = mul(qh, kh, NT) * each ** (-0.5) + bias[head]
        gate = jax.nn.sigmoid(score)
        weight = halves(score * gate * allowed)
        bend = gate * (1.0 + score * (1.0 - gate)) * allowed
        mixed.append(mul(weight, vh))
        kept.append((vh, qh, kh, weight, bend))
    yn, y_scale = norm_of(jnp.concatenate(mixed, axis=1))
    out = mul(halves(yn * upart), w_out) + emb
    states, s_scale = unit_of(out)
    united, e_scale = unit_of(emb)
    last = rows((count, width)) == count - 1
    target = jnp.where(last, 0.0, pltpu.roll(united, count - 1, 0))
    positive = sum_last(states * target) * (1.0 / TEMPER)
    expos = jnp.exp(positive)
    state_parts = halves(states)
    zneg = jnp.zeros((count, 1), F32)
    pulled = jnp.zeros((count, width), F32)
    for piece in packed:
        panel = halves(piece[count:])
        exps = jnp.exp(mul(state_parts, panel, NT) * (1.0 / TEMPER))
        zneg = zneg + sum_last(exps)
        pulled = pulled + mul(halves(exps), panel)
    total = expos + zneg
    loss = valid * (jnp.log(total) - positive)
    loss_ref[...] = jnp.sum(jnp.where(place_i == place_j, loss, 0.0), axis=0, keepdims=True)
    share = valid * (expos / total - 1.0) * (1.0 / TEMPER)
    d_states = share * target + pulled * (valid / total * (1.0 / TEMPER))
    d_out = unit_back(d_states, states, s_scale)
    first = rows((count, width)) == 0
    d_next = jnp.where(first, 0.0, pltpu.roll(share * states, 1, 0))
    d_emb = d_out + unit_back(d_next, united, e_scale)
    d_gated = mul(halves(d_out), w_out, NT)
    d_mixed = norm_back(d_gated * upart, yn, y_scale)
    d_hidden = [d_gated * yn]
    d_v, d_q, d_k = [], [], []
    for head in range(heads):
        vh, qh, kh, weight, bend = kept[head]
        d_mh = halves(d_mixed[:, each * head : each * (head + 1)])
        d_v.append(mul(weight, d_mh, TN))
        d_score = halves(mul(d_mh, vh, NT) * bend * each ** (-0.5))
        d_q.append(mul(d_score, kh))
        d_k.append(mul(d_score, qh, TN))
    d_pre = jnp.concatenate(d_hidden + d_v + d_q + d_k, axis=1) * slope
    d_xn = mul(halves(d_pre), w_in, NT)
    d_emb = d_emb + norm_back(d_xn, xn, x_scale)
    if len(grads) == 1:
        grads[0][...] = d_emb
        return
    whole[...] = d_emb
    part = width // len(grads)
    for step, out_ref in enumerate(grads):
        start = pl.multiple_of(partner(where, step, len(grads)) * part, part)
        out_ref[...] = whole[:, pl.ds(start, part)]


def layer(packed, lengths, weights, b_in, bias, where, parts):
    heads, count, _ = bias.shape
    in_h, in_l, out_h, out_l = weights
    width = in_h.shape[0]
    sds = jax.ShapeDtypeStruct
    return pl.pallas_call(
        functools.partial(layer_kernel, len(packed)),
        out_shape=(sds((1, count), F32),) + (sds((count, width // parts), F32),) * parts,
        in_specs=[SMEM, SMEM] + [VMEM] * (len(packed) + 6),
        out_specs=(VMEM,) * (1 + parts),
        scratch_shapes=[pltpu.VMEM((count, width), F32)],
        compiler_params=PARAMS,
        cost_estimate=pl.CostEstimate(
            flops=2_500_000_000, bytes_accessed=8_000_000, transcendentals=400_000
        ),
        name="layer",
    )(where.reshape(1), lengths, *packed, in_h, in_l, b_in.reshape(1, -1), out_h, out_l, bias)


def fetch_kernel(where, ids, neg_ids, *refs):
    packed_own, packed_other = refs[-2:]
    shards = refs[:-2]
    count = ids.shape[1]
    nrows = shards[0].shape[0]
    nneg = neg_ids.shape[1]
    me, other = (spread(ids[row : row + 1, :], count) for row in (0, 1))
    column = lanes((count, nrows))
    total = jnp.zeros((2 * count, shards[0].shape[1]), F32)
    for step, shard in enumerate(shards):
        base = where[step] * nrows
        hot = jnp.concatenate([me, other], 0) - base
        hot = jnp.where(hot == lanes(hot.shape), 1.0, 0.0).astype(BF16)
        total = total + pick(hot, shard[...])
        wanted = neg_ids[step : step + 1, :] - base
        chosen = jnp.where(rows((nrows, nneg)) == wanted, 1.0, 0.0).astype(BF16)
        chosen, _ = unit_of(pick(chosen, shard[...], TN))
        packed_own[count + nneg * step : count + nneg * (step + 1), :] = chosen
        packed_other[count + nneg * step : count + nneg * (step + 1), :] = chosen
    packed_own[:count, :] = total[:count]
    packed_other[:count, :] = total[count:]


def fetch(where, ids, neg_ids, shards):
    count = ids.shape[1]
    nneg = neg_ids.shape[1]
    width = shards[0].shape[1]
    shape = jax.ShapeDtypeStruct((count + nneg * len(shards), width), F32)
    return pl.pallas_call(
        fetch_kernel,
        out_shape=(shape, shape),
        in_specs=[SMEM] + [VMEM] * (2 + len(shards)),
        out_specs=(VMEM, VMEM),
        compiler_params=PARAMS,
        cost_estimate=pl.CostEstimate(flops=500_000_000, bytes_accessed=3_000_000, transcendentals=0),
        name="fetch",
    )(where, ids, neg_ids, *shards)


def gather_kernel(nrows, where, ids, *refs):
    own_ref, other_ref = refs[-2:]
    grads = refs[:-2]
    count = ids.shape[1]
    tokens = [halves(grad[...]) for grad in grads]
    high = jnp.concatenate([pair[0] for pair in tokens], 0)
    low = jnp.concatenate([pair[1] for pair in tokens], 0)
    names = jnp.concatenate([ids[row : row + 1, :] for row in range(len(grads))], 1)
    chips = where.shape[0] // 2
    for side, out_ref in ((0, own_ref), (1, other_ref)):
        for step in range(chips):
            base = where[side * chips + step] * nrows
            hot = rows((nrows, names.shape[1])) + base == names
            hot = jnp.where(hot, 1.0, 0.0).astype(BF16)
            dot = functools.partial(lax.dot_general, dimension_numbers=NN, preferred_element_type=F32)
            out_ref[nrows * step : nrows * (step + 1), :] = dot(hot, high) + dot(hot, low)


def gather(where, ids, grads, nrows):
    chips = where.shape[0] // 2
    shape = jax.ShapeDtypeStruct((chips * nrows, grads[0].shape[1]), F32)
    return pl.pallas_call(
        functools.partial(gather_kernel, nrows),
        out_shape=(shape, shape),
        in_specs=[SMEM] + [VMEM] * (1 + len(grads)),
        out_specs=(VMEM, VMEM),
        compiler_params=PARAMS,
        cost_estimate=pl.CostEstimate(flops=300_000_000, bytes_accessed=1_000_000, transcendentals=0),
        name="gather",
    )(where, ids, *grads)


def partner(index, step, size):
    if size & (size - 1) == 0:
        return index ^ step
    return (index + step) % size


def swap(value, axis, step, size):
    return lax.ppermute(value, axis, [(i, i ^ step) for i in range(size)])


def direct(item_ids, neg_ids, lengths, table, weights, b_in, bias):
    groups = lax.axis_size("group")
    shards = lax.axis_size("shard")
    plane = lax.axis_index("shard")
    group = lax.axis_index("group")
    chips = groups // 2
    nrows, width = table.shape
    own_side = [group ^ (2 * step) for step in range(chips)]
    where = jnp.stack(own_side + [index ^ 1 for index in own_side]).astype(jnp.int32)
    item_row = item_ids.reshape(1, -1)
    neg_row = neg_ids.reshape(1, -1)
    panels = [table] + [swap(table, "group", 2 * step, groups) for step in range(1, chips)]
    neg_rows = [neg_row] + [swap(neg_row, "group", 2 * step, groups) for step in range(1, chips)]
    pair = jnp.concatenate([item_row, swap(item_row, "group", 1, groups)], 0)
    names = jnp.concatenate(
        [item_row] + [swap(item_row, "shard", step, shards) for step in range(1, shards)], 0
    )
    mine, theirs = fetch(where, pair, jnp.concatenate(neg_rows, 0), panels)
    theirs = swap(theirs, "group", 1, groups)
    loss, *grads = layer([mine, theirs], lengths, weights, b_in, bias, plane, shards)
    blocks = [grads[0]] + [swap(grads[step], "shard", step, shards) for step in range(1, shards)]
    own, other = gather(where, names, blocks, nrows)
    own = own + swap(other, "group", 1, groups)
    own = own.reshape(chips, nrows, -1)
    total = own[0]
    for step in range(1, chips):
        total = total + swap(own[step], "group", 2 * step, groups)
    columns = [total] + [swap(total, "shard", step, shards) for step in range(1, shards)]
    stacked = jnp.stack(columns)
    order = jnp.arange(shards, dtype=jnp.int32) ^ plane
    table_grad = jnp.concatenate(
        [lax.dynamic_index_in_dim(stacked, order[step], 0, False) for step in range(shards)], 1
    )
    return table_grad, loss


def picker_of(wanted, rows_dev):
    flat = wanted.reshape(-1)
    return (flat[:, None] == jnp.arange(rows_dev, dtype=jnp.int32)[None, :]).astype(F32)


def by_request(item_ids, neg_ids, lengths, table, weights, b_in, bias):
    high = lax.Precision.HIGHEST
    groups = lax.axis_size("group")
    rows_dev, width = table.shape
    count = item_ids.shape[0]
    capacity = max(2, 2 * count // groups)
    slots = groups * capacity
    owner = item_ids // rows_dev
    member = (owner[:, None] == jnp.arange(groups, dtype=jnp.int32)[None, :]).astype(jnp.int32)
    rank = jnp.sum(member * (jnp.cumsum(member, 0) - 1), 1)
    target_slot = owner * capacity + rank
    requests = (
        jnp.full((slots,), -1, jnp.int32)
        .at[target_slot]
        .set(item_ids % rows_dev)
        .reshape(groups, capacity)
    )
    own_negatives, _ = unit_of(table[neg_ids.reshape(-1) % rows_dev])
    panel_rows = lax.all_gather(own_negatives, "group", axis=0, tiled=True)
    incoming = lax.all_to_all(requests, "group", split_axis=0, concat_axis=0, tiled=True)
    picker = picker_of(incoming, rows_dev)
    served = jnp.dot(picker, table, precision=high).reshape(groups, capacity, width)
    returned = lax.all_to_all(served, "group", split_axis=0, concat_axis=0, tiled=True)
    emb = returned.reshape(slots, width)[target_slot]
    packed = jnp.concatenate([emb, panel_rows], 0)
    loss, d_emb = layer([packed], lengths, weights, b_in, bias, jnp.int32(0), 1)
    outgoing = jnp.zeros((slots, width), F32).at[target_slot].set(d_emb)
    arrived = lax.all_to_all(
        outgoing.reshape(groups, capacity, width), "group", split_axis=0, concat_axis=0, tiled=True
    )
    partial_grad = jnp.dot(picker.T, arrived.reshape(slots, width), precision=high)
    return lax.psum(partial_grad, "shard"), loss


def body(item_ids, seq_lengths, time_buckets, neg_ids, table, w_in, b_in, w_out, rab):
    groups = lax.axis_size("group")
    shards = lax.axis_size("shard")
    width = table.shape[1]
    *weights, bias = prepare(w_in, w_out, rab, time_buckets)
    small = groups <= 16 and groups & (groups - 1) == 0 and shards * LANES == width
    plan = direct if small and groups > 1 else by_request
    grad, loss = plan(item_ids, neg_ids, seq_lengths, table, weights, b_in, bias)
    return grad, loss.reshape(-1)


def solution(mesh):
    in_specs = (
        P(("shard", "group")),
        P(("shard", "group"), None),
        P(("shard", "group")),
        P("shard", "group"),
        P("group", None),
        P(),
        P(),
        P(),
        P(),
    )
    out_specs = (P("group", None), P(("shard", "group")))
    return jax.shard_map(body, mesh=mesh, in_specs=in_specs, out_specs=out_specs, check_vma=False)
```

```python
import functools

import jax
import jax.numpy as jnp
from jax import lax
from jax.experimental import pallas as pl
from jax.experimental.pallas import tpu as pltpu
from jax.sharding import PartitionSpec as P

MOST_LEN = 64
TEMPER = 0.05
LANES = 128
SUBLANES = 8
F32 = jnp.float32
BF16 = jnp.bfloat16
NN = (((1,), (0,)), ((), ()))
NT = (((1,), (1,)), ((), ()))
TN = (((0,), (0,)), ((), ()))
VMEM = pl.BlockSpec(memory_space=pltpu.VMEM)
SMEM = pl.BlockSpec(memory_space=pltpu.SMEM)


def limit(mebibytes):
    return pltpu.CompilerParams(vmem_limit_bytes=mebibytes * 1024 * 1024)


def halves(value):
    high = value.astype(BF16)
    return high, (value - high.astype(F32)).astype(BF16)


def mul(left, right, dims=NN):
    lh, ll = left
    rh, rl = right
    dot = functools.partial(lax.dot_general, dimension_numbers=dims, preferred_element_type=F32)
    return dot(lh, rh) + (dot(ll, rh) + dot(lh, rl))


def pick(hot, value, dims=NN):
    high = value.astype(BF16)
    rest = value - high.astype(F32)
    mid = rest.astype(BF16)
    low = (rest - mid.astype(F32)).astype(BF16)
    dot = functools.partial(lax.dot_general, dimension_numbers=dims, preferred_element_type=F32)
    return dot(hot, high) + (dot(hot, mid) + dot(hot, low))


def sum_last(value):
    return jnp.sum(value, axis=-1, keepdims=True)


def mean_last(value):
    return jnp.mean(value, axis=-1, keepdims=True)


def lanes(shape):
    return lax.broadcasted_iota(jnp.int32, shape, 1)


def rows(shape):
    return lax.broadcasted_iota(jnp.int32, shape, 0)


def spread(row, count):
    wide = jnp.broadcast_to(row.astype(F32), (count, count))
    return wide.T.astype(jnp.int32)


def norm_of(value):
    centered = value - mean_last(value)
    scale = lax.rsqrt(mean_last(centered * centered) + 1e-05)
    return centered * scale, scale


def norm_back(grad, normed, scale):
    return scale * (grad - mean_last(grad) - normed * mean_last(grad * normed))


def unit_of(value):
    scale = lax.rsqrt(sum_last(value * value) + 1e-06)
    return value * scale, scale


def unit_back(grad, united, scale):
    return scale * (grad - united * sum_last(grad * united))


def time_bias(rab, buckets, bias):
    count = buckets.shape[1]
    mine = jnp.broadcast_to(buckets[...], (count, count))
    gap = jnp.abs(mine - spread(buckets[...], count))
    heads, nbuck = rab.shape
    for head in range(heads):
        level = jnp.concatenate([rab[head : head + 1, :], jnp.zeros((1, LANES - nbuck), F32)], 1)
        level = jnp.broadcast_to(level, (count, LANES))
        bias[head] = jnp.take_along_axis(level, gap, axis=1)


def prepare_kernel(w_in, w_out, rab, buckets, in_h, in_l, out_h, out_l, bias):
    in_h[...], in_l[...] = halves(w_in[...])
    out_h[...], out_l[...] = halves(w_out[...])
    time_bias(rab, buckets, bias)


def prepare_own_kernel(
    where, w_in, w_out, rab, buckets, ids, wanted, table, in_h, in_l, out_h, out_l, bias, hot, rows_ref, panel
):
    prepare_kernel(w_in, w_out, rab, buckets, in_h, in_l, out_h, out_l, bias)
    count = ids.shape[1]
    me, other = (spread(ids[row : row + 1, :], count) for row in (0, 1))
    hot[:count] = me
    hot[count:] = other
    rows_ref[...], panel[...] = chosen_rows(where[0], hot[...], wanted[...], table[...])


def prepare(w_in, w_out, rab, buckets, extra=()):
    count = buckets.shape[0]
    width, hidden = w_in.shape
    heads = rab.shape[0]
    sds = jax.ShapeDtypeStruct
    outs = (
        sds((width, hidden), BF16),
        sds((width, hidden), BF16),
        sds((width, width), BF16),
        sds((width, width), BF16),
        sds((heads, count, count), F32),
    )
    kernel, first, specs = prepare_kernel, (), ()
    if extra:
        where, *extra = extra
        kernel, first, specs = prepare_own_kernel, (where,), (SMEM,)
        nneg = extra[1].shape[1]
        outs += (
            sds((2 * count, count), jnp.int32),
            sds((2 * count, width), F32),
            sds((nneg, width), F32),
        )
    return pl.pallas_call(
        kernel,
        out_shape=outs,
        in_specs=list(specs) + [VMEM] * (4 + len(extra)),
        out_specs=(VMEM,) * len(outs),
        compiler_params=limit(8),
        cost_estimate=pl.CostEstimate(flops=200_000_000, bytes_accessed=12_000_000, transcendentals=0),
        name="prepare",
    )(*first, w_in, w_out, rab, buckets.reshape(1, count), *extra)


def layer_kernel(pieces, where, lengths, *refs):
    plane = where[where.shape[0] - 1]
    packed = refs[:pieces]
    in_h, in_l, b_in, out_h, out_l, bias, ids = refs[pieces : pieces + 7]
    loss_ref = refs[pieces + 7]
    grads = refs[pieces + 8 : -1]
    whole = refs[-1]
    heads, count, _ = bias.shape
    width = in_h.shape[0]
    each = width // heads
    emb = packed[0][:count]
    for other in packed[1:]:
        emb = emb + other[:count]
    square = (count, count)
    seg_i = jnp.zeros(square, jnp.int32)
    seg_j = jnp.zeros(square, jnp.int32)
    seg_n = jnp.zeros((count, 1), jnp.int32)
    place_i, place_j, place = rows(square), lanes(square), rows((count, 1))
    end = jnp.int32(0)
    for index in range(lengths.shape[1]):
        end = end + lengths[0, index]
        seg_i = seg_i + (place_i >= end).astype(jnp.int32)
        seg_j = seg_j + (place_j >= end).astype(jnp.int32)
        seg_n = seg_n + (place + 1 >= end).astype(jnp.int32)
    allowed = jnp.where((place_j <= place_i) & (seg_i == seg_j), 1.0 / MOST_LEN, 0.0).astype(F32)
    valid = jnp.where((seg_n == seg_i[:, :1]) & (place + 1 < count), 1.0, 0.0).astype(F32)
    xn, x_scale = norm_of(emb)
    w_in = (in_h[...], in_l[...])
    w_out = (out_h[...], out_l[...])
    pre = mul(halves(xn), w_in) + b_in[...]
    sig = jax.nn.sigmoid(pre)
    hidden = pre * sig
    slope = sig * (1.0 + pre * (1.0 - sig))
    upart = hidden[:, :width]
    kept = []
    mixed = []
    for head in range(heads):
        vh, qh, kh = (
            halves(hidden[:, width * part + each * head : width * part + each * (head + 1)])
            for part in (1, 2, 3)
        )
        score = mul(qh, kh, NT) * each ** (-0.5) + bias[head]
        gate = jax.nn.sigmoid(score)
        weight = halves(score * gate * allowed)
        bend = gate * (1.0 + score * (1.0 - gate)) * allowed
        mixed.append(mul(weight, vh))
        kept.append((vh, qh, kh, weight, bend))
    yn, y_scale = norm_of(jnp.concatenate(mixed, axis=1))
    out = mul(halves(yn * upart), w_out) + emb
    states, s_scale = unit_of(out)
    united, e_scale = unit_of(emb)
    last = rows((count, width)) == count - 1
    target = jnp.where(last, 0.0, pltpu.roll(united, count - 1, 0))
    positive = sum_last(states * target) * (1.0 / TEMPER)
    expos = jnp.exp(positive)
    state_parts = halves(states)
    zneg = jnp.zeros((count, 1), F32)
    pulled = jnp.zeros((count, width), F32)
    for piece in packed:
        panel = halves(piece[count:])
        exps = jnp.exp(mul(state_parts, panel, NT) * (1.0 / TEMPER))
        zneg = zneg + sum_last(exps)
        pulled = pulled + mul(halves(exps), panel)
    total = expos + zneg
    loss = valid * (jnp.log(total) - positive)
    loss_ref[...] = jnp.sum(jnp.where(place_i == place_j, loss, 0.0), axis=0, keepdims=True)
    share = valid * (expos / total - 1.0) * (1.0 / TEMPER)
    d_states = share * target + pulled * (valid / total * (1.0 / TEMPER))
    d_out = unit_back(d_states, states, s_scale)
    first = rows((count, width)) == 0
    d_next = jnp.where(first, 0.0, pltpu.roll(share * states, 1, 0))
    d_emb = d_out + unit_back(d_next, united, e_scale)
    d_gated = mul(halves(d_out), w_out, NT)
    d_mixed = norm_back(d_gated * upart, yn, y_scale)
    d_hidden = [d_gated * yn]
    d_v, d_q, d_k = [], [], []
    for head in range(heads):
        vh, qh, kh, weight, bend = kept[head]
        d_mh = halves(d_mixed[:, each * head : each * (head + 1)])
        d_v.append(mul(weight, d_mh, TN))
        d_score = halves(mul(d_mh, vh, NT) * bend * each ** (-0.5))
        d_q.append(mul(d_score, kh))
        d_k.append(mul(d_score, qh, TN))
    d_pre = jnp.concatenate(d_hidden + d_v + d_q + d_k, axis=1) * slope
    d_xn = mul(halves(d_pre), w_in, NT)
    d_emb = d_emb + norm_back(d_xn, xn, x_scale)
    if len(grads) == 1:
        grads[0][...] = d_emb
        return
    whole[...] = d_emb
    part = width // len(grads)
    for step, out_ref in enumerate(grads):
        start = pl.multiple_of((plane ^ step) * part, part)
        out_ref[:count] = whole[:, pl.ds(start, part)]
        out_ref[count:] = jnp.broadcast_to(ids[...].astype(F32), (SUBLANES, part))


def layer(packed, lengths, weights, b_in, bias, ids, where, parts):
    heads, count, _ = bias.shape
    extra = SUBLANES if parts > 1 else 0
    in_h, in_l, out_h, out_l = weights
    width = in_h.shape[0]
    sds = jax.ShapeDtypeStruct
    return pl.pallas_call(
        functools.partial(layer_kernel, len(packed)),
        out_shape=(sds((1, count), F32),) + (sds((count + extra, width // parts), F32),) * parts,
        in_specs=[SMEM, SMEM] + [VMEM] * (len(packed) + 7),
        out_specs=(VMEM,) * (1 + parts),
        scratch_shapes=[pltpu.VMEM((count, width), F32)],
        compiler_params=limit(14 if parts > 1 else 40),
        cost_estimate=pl.CostEstimate(
            flops=2_500_000_000, bytes_accessed=8_000_000, transcendentals=400_000
        ),
        name="layer",
    )(where, lengths, *packed, in_h, in_l, b_in.reshape(1, -1), out_h, out_l, bias, ids)


def pack_kernel(neg_ids, table, out_ref, ids, sems):
    nrows, width = table.shape
    body_copy = pltpu.make_async_copy(table, out_ref.at[pl.ds(0, nrows)], sems.at[0])
    body_copy.start()
    id_copy = pltpu.make_async_copy(neg_ids, ids, sems.at[1])
    id_copy.start()
    id_copy.wait()
    tail = jnp.zeros((1, width - ids.shape[1]), F32)
    row = jnp.concatenate([ids[...].astype(F32), tail], 1)
    out_ref[nrows:] = jnp.broadcast_to(row, (SUBLANES, width))
    body_copy.wait()


def pack(neg_ids, table):
    nrows, width = table.shape
    return pl.pallas_call(
        pack_kernel,
        out_shape=jax.ShapeDtypeStruct((nrows + SUBLANES, width), F32),
        in_specs=[pl.BlockSpec(memory_space=pl.ANY)] * 2,
        out_specs=VMEM,
        scratch_shapes=[pltpu.VMEM(neg_ids.shape, jnp.int32), pltpu.SemaphoreType.DMA((2,))],
        compiler_params=limit(4),
        cost_estimate=pl.CostEstimate(flops=0, bytes_accessed=600_000, transcendentals=0),
        name="pack",
    )(neg_ids, table)


def chosen_rows(owner, items, wanted, held):
    nrows = held.shape[0]
    base = owner * nrows
    hot = jnp.where(items - base == lanes(items.shape), 1.0, 0.0).astype(BF16)
    chosen = jnp.where(rows((nrows, wanted.shape[1])) == wanted - base, 1.0, 0.0).astype(BF16)
    return pick(hot, held), unit_of(pick(chosen, held, TN))[0]


def fetch_kernel(where, items, partial, panel, *refs):
    packed_own, packed_other = refs[-2:]
    shards = refs[:-2]
    nneg = panel.shape[0]
    count = packed_own.shape[0] - nneg * (1 + len(shards))
    total = partial[...]
    packed_own[count : count + nneg, :] = panel[...]
    packed_other[count : count + nneg, :] = panel[...]
    for step, shard in enumerate(shards, 1):
        nrows = shard.shape[0] - SUBLANES
        wanted = shard[nrows : nrows + 1, :nneg].astype(jnp.int32)
        found, chosen = chosen_rows(where[step], items[...], wanted, shard[:nrows])
        total = total + found
        packed_own[count + nneg * step : count + nneg * (step + 1), :] = chosen
        packed_other[count + nneg * step : count + nneg * (step + 1), :] = chosen
    packed_own[:count, :] = total[:count]
    packed_other[:count, :] = total[count:]


def fetch(where, items, partial, panel, shards):
    nneg, width = panel.shape
    count = items.shape[1]
    shape = jax.ShapeDtypeStruct((count + nneg * (1 + len(shards)), width), F32)
    return pl.pallas_call(
        fetch_kernel,
        out_shape=(shape, shape),
        in_specs=[SMEM] + [VMEM] * (3 + len(shards)),
        out_specs=(VMEM, VMEM),
        compiler_params=limit(4),
        cost_estimate=pl.CostEstimate(flops=500_000_000, bytes_accessed=3_000_000, transcendentals=0),
        name="fetch",
    )(where, items, partial, panel, *shards)


def gather_kernel(nrows, where, *refs):
    own_ref, other_ref = refs[-2:]
    grads = refs[:-2]
    count = grads[0].shape[0] - SUBLANES
    tokens = [halves(grad[:count]) for grad in grads]
    high = jnp.concatenate([pair[0] for pair in tokens], 0)
    low = jnp.concatenate([pair[1] for pair in tokens], 0)
    names = jnp.concatenate([grad[count : count + 1] for grad in grads], 1).astype(jnp.int32)
    chips = own_ref.shape[0] // nrows
    for side, out_ref in ((0, own_ref), (1, other_ref)):
        for step in range(chips):
            base = where[side * chips + step] * nrows
            hot = rows((nrows, names.shape[1])) + base == names
            hot = jnp.where(hot, 1.0, 0.0).astype(BF16)
            dot = functools.partial(lax.dot_general, dimension_numbers=NN, preferred_element_type=F32)
            out_ref[nrows * step : nrows * (step + 1), :] = dot(hot, high) + dot(hot, low)


def gather(where, grads, nrows, chips):
    shape = jax.ShapeDtypeStruct((chips * nrows, grads[0].shape[1]), F32)
    return pl.pallas_call(
        functools.partial(gather_kernel, nrows),
        out_shape=(shape, shape),
        in_specs=[SMEM] + [VMEM] * len(grads),
        out_specs=(VMEM, VMEM),
        compiler_params=limit(4),
        cost_estimate=pl.CostEstimate(flops=300_000_000, bytes_accessed=1_000_000, transcendentals=0),
        name="gather",
    )(where, *grads)


def join_kernel(where, *refs):
    plane = where[where.shape[0] - 1]
    out_ref = refs[-1]
    for step, block in enumerate(refs[:-1]):
        part = block.shape[1]
        start = pl.multiple_of((plane ^ step) * part, part)
        out_ref[:, pl.ds(start, part)] = block[...]


def join(where, blocks):
    nrows, part = blocks[0].shape
    return pl.pallas_call(
        join_kernel,
        out_shape=jax.ShapeDtypeStruct((nrows, part * len(blocks)), F32),
        in_specs=[SMEM] + [VMEM] * len(blocks),
        out_specs=VMEM,
        compiler_params=limit(4),
        cost_estimate=pl.CostEstimate(flops=0, bytes_accessed=500_000, transcendentals=0),
        name="join",
    )(where, *blocks)


def swap(value, axis, step, size):
    return lax.ppermute(value, axis, [(i, i ^ step) for i in range(size)])


def direct(item_ids, lengths, buckets, neg_ids, table, w_in, b_in, w_out, rab):
    groups = lax.axis_size("group")
    shards = lax.axis_size("shard")
    group = lax.axis_index("group")
    chips = groups // 2
    nrows = table.shape[0]
    own_side = [group ^ (2 * step) for step in range(chips)]
    scalars = own_side + [index ^ 1 for index in own_side] + [lax.axis_index("shard")]
    where = jnp.stack(scalars).astype(jnp.int32)
    item_row = item_ids.reshape(1, -1)
    neg_row = neg_ids.reshape(1, -1)
    packed = pack(neg_row, table)
    panels = [swap(packed, "group", 2 * step, groups) for step in range(1, chips)]
    pair = jnp.concatenate([item_row, swap(item_row, "group", 1, groups)], 0)
    *weights, bias, items, partial, panel = prepare(
        w_in, w_out, rab, buckets, (where, pair, neg_row, table)
    )
    mine, theirs = fetch(where, items, partial, panel, panels)
    theirs = swap(theirs, "group", 1, groups)
    loss, *grads = layer([mine, theirs], lengths, weights, b_in, bias, item_row, where, shards)
    blocks = [grads[0]] + [swap(grads[step], "shard", step, shards) for step in range(1, shards)]
    own, other = gather(where, blocks, nrows, chips)
    own = own + swap(other, "group", 1, groups)
    own = own.reshape(chips, nrows, -1)
    total = own[0]
    for step in range(1, chips):
        total = total + swap(own[step], "group", 2 * step, groups)
    columns = [total] + [swap(total, "shard", step, shards) for step in range(1, shards)]
    return join(where, columns), loss


def picker_of(wanted, rows_dev):
    flat = wanted.reshape(-1)
    return (flat[:, None] == jnp.arange(rows_dev, dtype=jnp.int32)[None, :]).astype(F32)


def by_request(item_ids, lengths, buckets, neg_ids, table, w_in, b_in, w_out, rab):
    high = lax.Precision.HIGHEST
    *weights, bias = prepare(w_in, w_out, rab, buckets)
    groups = lax.axis_size("group")
    rows_dev, width = table.shape
    count = item_ids.shape[0]
    capacity = max(2, 2 * count // groups)
    slots = groups * capacity
    owner = item_ids // rows_dev
    member = (owner[:, None] == jnp.arange(groups, dtype=jnp.int32)[None, :]).astype(jnp.int32)
    rank = jnp.sum(member * (jnp.cumsum(member, 0) - 1), 1)
    target_slot = owner * capacity + rank
    requests = (
        jnp.full((slots,), -1, jnp.int32)
        .at[target_slot]
        .set(item_ids % rows_dev)
        .reshape(groups, capacity)
    )
    own_negatives, _ = unit_of(table[neg_ids.reshape(-1) % rows_dev])
    panel_rows = lax.all_gather(own_negatives, "group", axis=0, tiled=True)
    incoming = lax.all_to_all(requests, "group", split_axis=0, concat_axis=0, tiled=True)
    picker = picker_of(incoming, rows_dev)
    served = jnp.dot(picker, table, precision=high).reshape(groups, capacity, width)
    returned = lax.all_to_all(served, "group", split_axis=0, concat_axis=0, tiled=True)
    emb = returned.reshape(slots, width)[target_slot]
    packed = jnp.concatenate([emb, panel_rows], 0)
    loss, d_emb = layer(
        [packed], lengths, weights, b_in, bias, item_ids.reshape(1, -1), jnp.zeros((1,), jnp.int32), 1
    )
    outgoing = jnp.zeros((slots, width), F32).at[target_slot].set(d_emb)
    arrived = lax.all_to_all(
        outgoing.reshape(groups, capacity, width), "group", split_axis=0, concat_axis=0, tiled=True
    )
    partial_grad = jnp.dot(picker.T, arrived.reshape(slots, width), precision=high)
    return lax.psum(partial_grad, "shard"), loss


def body(item_ids, seq_lengths, time_buckets, neg_ids, table, w_in, b_in, w_out, rab):
    groups = lax.axis_size("group")
    shards = lax.axis_size("shard")
    width = table.shape[1]
    small = groups in (2, 4, 8, 16) and shards & (shards - 1) == 0 and shards > 1
    small = small and item_ids.shape[0] == LANES and shards * LANES == width
    plan = direct if small else by_request
    grad, loss = plan(
        item_ids, seq_lengths, time_buckets, neg_ids, table, w_in, b_in, w_out, rab
    )
    return grad, loss.reshape(-1)


def solution(mesh):
    in_specs = (
        P(("shard", "group")),
        P(("shard", "group"), None),
        P(("shard", "group")),
        P("shard", "group"),
        P("group", None),
        P(),
        P(),
        P(),
        P(),
    )
    out_specs = (P("group", None), P(("shard", "group")))
    return jax.shard_map(body, mesh=mesh, in_specs=in_specs, out_specs=out_specs, check_vma=False)
```

```python
import functools

import jax
import jax.numpy as jnp
from jax import lax
from jax.experimental import pallas as pl
from jax.experimental.pallas import tpu as pltpu
from jax.sharding import PartitionSpec as P

MOST_LEN = 64
TEMPER = 0.05
LANES = 128
SUBLANES = 8
F32 = jnp.float32
BF16 = jnp.bfloat16
NN = (((1,), (0,)), ((), ()))
NT = (((1,), (1,)), ((), ()))
TN = (((0,), (0,)), ((), ()))
VMEM = pl.BlockSpec(memory_space=pltpu.VMEM)
SMEM = pl.BlockSpec(memory_space=pltpu.SMEM)


def limit(mebibytes):
    return pltpu.CompilerParams(vmem_limit_bytes=mebibytes * 1024 * 1024)


def halves(value):
    high = value.astype(BF16)
    return high, (value - high.astype(F32)).astype(BF16)


def mul(left, right, dims=NN):
    lh, ll = left
    rh, rl = right
    dot = functools.partial(lax.dot_general, dimension_numbers=dims, preferred_element_type=F32)
    both = dot(jnp.concatenate([lh, ll], 0), rh)
    count = lh.shape[0]
    return both[:count] + (both[count:] + dot(lh, rl))


def sum_last(value):
    return jnp.sum(value, axis=-1, keepdims=True)


def mean_last(value):
    return jnp.mean(value, axis=-1, keepdims=True)


def lanes(shape):
    return lax.broadcasted_iota(jnp.int32, shape, 1)


def rows(shape):
    return lax.broadcasted_iota(jnp.int32, shape, 0)


def spread(row, count):
    wide = jnp.broadcast_to(row.astype(F32), (count, count))
    return wide.T.astype(jnp.int32)


def column(row):
    short = LANES - row.shape[1]
    if short:
        row = jnp.concatenate([row, jnp.full((1, short), -1, jnp.int32)], 1)
    return spread(row, LANES)


def norm_of(value):
    centered = value - mean_last(value)
    scale = lax.rsqrt(mean_last(centered * centered) + 1e-05)
    return centered * scale, scale


def norm_back(grad, normed, scale):
    return scale * (grad - mean_last(grad) - normed * mean_last(grad * normed))


def unit_of(value):
    scale = lax.rsqrt(sum_last(value * value) + 1e-06)
    return value * scale, scale


def unit_back(grad, united, scale):
    return scale * (grad - united * sum_last(grad * united))


def time_bias(rab, buckets, bias):
    count = buckets.shape[1]
    mine = jnp.broadcast_to(buckets[...], (count, count))
    gap = jnp.abs(mine - spread(buckets[...], count))
    heads, nbuck = rab.shape
    for head in range(heads):
        level = jnp.concatenate([rab[head : head + 1, :], jnp.zeros((1, LANES - nbuck), F32)], 1)
        level = jnp.broadcast_to(level, (count, LANES))
        bias[head] = jnp.take_along_axis(level, gap, axis=1)


def masks(lengths, count):
    square = (count, count)
    seg_i = jnp.zeros(square, jnp.int32)
    seg_j = jnp.zeros(square, jnp.int32)
    seg_n = jnp.zeros(square, jnp.int32)
    place_i, place_j = rows(square), lanes(square)
    end = jnp.int32(0)
    for index in range(lengths.shape[1]):
        end = end + lengths[0, index]
        seg_i = seg_i + (place_i >= end).astype(jnp.int32)
        seg_j = seg_j + (place_j >= end).astype(jnp.int32)
        seg_n = seg_n + (place_i + 1 >= end).astype(jnp.int32)
    allowed = jnp.where((place_j <= place_i) & (seg_i == seg_j), 1.0 / MOST_LEN, 0.0)
    valid = jnp.where((seg_n == seg_i) & (place_i + 1 < count), 1.0, 0.0)
    return allowed.astype(F32), valid.astype(F32)


def prepare_kernel(
    lengths, w_in, w_out, rab, buckets, in_h, in_l, in_th, in_tl, out_h, out_l, out_th, out_tl, bias, allowed, valid
):
    width, hidden = w_in.shape
    allowed[...], valid[...] = masks(lengths, allowed.shape[0])
    out_h[...], out_l[...] = halves(w_out[...])
    out_th[...], out_tl[...] = halves(w_out[...].T)
    for start in range(0, hidden, width):
        part = slice(start, start + width)
        in_h[:, part], in_l[:, part] = halves(w_in[:, part])
        in_th[part, :], in_tl[part, :] = halves(w_in[:, part].T)
    time_bias(rab, buckets, bias)


def prepare_own_kernel(
    where, lengths, w_in, w_out, rab, buckets, ids, wanted, table, *outs
):
    *weights, items, found, panel, spots = outs
    for index in range(where.shape[0]):
        spots[index : index + 1, :] = jnp.full((1, LANES), where[index], jnp.int32)
    prepare_kernel(lengths, w_in, w_out, rab, buckets, *weights)
    count = ids.shape[1]
    me, other = (spread(ids[row : row + 1, :], count) for row in (0, 1))
    items[:count] = me
    items[count:] = other
    nneg = panel.shape[0]
    names = jnp.concatenate([me, other, column(wanted[...])[:nneg]], 0)
    chosen = chosen_rows([where[0]], names, [table[...]])
    found[...] = chosen[: 2 * count]
    panel[...] = unit_of(chosen[2 * count :])[0]


def prepare(lengths, w_in, w_out, rab, buckets, extra=()):
    count = buckets.shape[0]
    width, hidden = w_in.shape
    heads = rab.shape[0]
    sds = jax.ShapeDtypeStruct
    outs = (
        *(sds((width, hidden), BF16),) * 2,
        *(sds((hidden, width), BF16),) * 2,
        *(sds((width, width), BF16),) * 4,
        sds((heads, count, count), F32),
        *(sds((count, count), F32),) * 2,
    )
    kernel, first, specs = prepare_kernel, (lengths,), (SMEM,)
    if extra:
        where, *extra = extra
        kernel, first, specs = prepare_own_kernel, (where, lengths), (SMEM, SMEM)
        nneg = extra[1].shape[1]
        outs += (
            sds((2 * count, count), jnp.int32),
            sds((2 * count, width), F32),
            sds((nneg, width), F32),
            sds((where.shape[0], LANES), jnp.int32),
        )
    return pl.pallas_call(
        kernel,
        out_shape=outs,
        in_specs=list(specs) + [VMEM] * (4 + len(extra)),
        out_specs=(VMEM,) * len(outs),
        compiler_params=limit(12),
        cost_estimate=pl.CostEstimate(flops=200_000_000, bytes_accessed=12_000_000, transcendentals=0),
        name="prepare",
    )(*first, w_in, w_out, rab, buckets.reshape(1, count), *extra)


def layer_kernel(pieces, spots, *refs):
    packed = refs[:pieces]
    in_h, in_l, in_th, in_tl, out_h, out_l, out_th, out_tl = refs[pieces : pieces + 8]
    b_in, bias, allowed_ref, valid_ref, ids = refs[pieces + 8 : pieces + 13]
    loss_ref = refs[pieces + 13]
    grads = refs[pieces + 14 :]
    heads, count, _ = bias.shape
    width = in_h.shape[0]
    each = width // heads
    emb = packed[0][:count]
    if pieces > 1:
        emb = emb + packed[2][...]
    allowed = allowed_ref[...]
    valid = valid_ref[:, :1]
    square = (count, count)
    place_i, place_j = rows(square), lanes(square)
    xn, x_scale = norm_of(emb)
    w_in = (in_h[...], in_l[...])
    w_out = (out_h[...], out_l[...])
    pre = mul(halves(xn), w_in) + b_in[...]
    sig = jax.nn.sigmoid(pre)
    hidden = pre * sig
    slope = sig * (1.0 + pre * (1.0 - sig))
    upart = hidden[:, :width]
    kept = []
    mixed = []
    for head in range(heads):
        vh, qh, kh = (
            halves(hidden[:, width * part + each * head : width * part + each * (head + 1)])
            for part in (1, 2, 3)
        )
        score = mul(qh, kh, NT) * each ** (-0.5) + bias[head]
        gate = jax.nn.sigmoid(score)
        weight = score * gate * allowed
        bend = gate * (1.0 + score * (1.0 - gate)) * allowed
        mixed.append(mul(halves(weight), vh))
        kept.append((vh, qh, kh, halves(weight.T), bend))
    yn, y_scale = norm_of(jnp.concatenate(mixed, axis=1))
    out = mul(halves(yn * upart), w_out) + emb
    states, s_scale = unit_of(out)
    united, e_scale = unit_of(emb)
    last = rows((count, width)) == count - 1
    target = jnp.where(last, 0.0, pltpu.roll(united, count - 1, 0))
    positive = sum_last(states * target) * (1.0 / TEMPER)
    expos = jnp.exp(positive)
    state_parts = halves(states)
    panel = halves(jnp.concatenate([piece[count:] for piece in packed[:2]], 0))
    exps = jnp.exp(mul(state_parts, panel, NT) * (1.0 / TEMPER))
    zneg = sum_last(exps)
    pulled = mul(halves(exps), panel)
    total = expos + zneg
    loss = valid * (jnp.log(total) - positive)
    loss_ref[...] = jnp.sum(jnp.where(place_i == place_j, loss, 0.0), axis=0, keepdims=True)
    share = valid * (expos / total - 1.0) * (1.0 / TEMPER)
    d_states = share * target + pulled * (valid / total * (1.0 / TEMPER))
    d_out = unit_back(d_states, states, s_scale)
    first = rows((count, width)) == 0
    d_next = jnp.where(first, 0.0, pltpu.roll(share * states, 1, 0))
    d_emb = d_out + unit_back(d_next, united, e_scale)
    d_gated = mul(halves(d_out), (out_th[...], out_tl[...]))
    d_mixed = norm_back(d_gated * upart, yn, y_scale)
    d_hidden = [d_gated * yn]
    d_v, d_q, d_k = [], [], []
    for head in range(heads):
        vh, qh, kh, weight_t, bend = kept[head]
        d_mh = halves(d_mixed[:, each * head : each * (head + 1)])
        d_v.append(mul(weight_t, d_mh))
        d_score = mul(d_mh, vh, NT) * bend * each ** (-0.5)
        d_q.append(mul(halves(d_score), kh))
        d_k.append(mul(halves(d_score.T), qh))
    d_pre = jnp.concatenate(d_hidden + d_v + d_q + d_k, axis=1) * slope
    d_xn = mul(halves(d_pre), (in_th[...], in_tl[...]))
    d_emb = d_emb + norm_back(d_xn, xn, x_scale)
    if len(grads) == 1:
        grads[0][...] = d_emb
        return
    part = width // len(grads)
    plane = spots[spots.shape[0] - 1 :, :part]
    for step, out_ref in enumerate(grads):
        block = d_emb[:, :part]
        for spot in range(1, len(grads)):
            mine = (plane ^ step) == spot
            block = jnp.where(mine, d_emb[:, part * spot : part * (spot + 1)], block)
        out_ref[:count] = block
        out_ref[count:] = jnp.broadcast_to(ids[...].astype(F32), (SUBLANES, part))


def layer(*packed, weights, b_in, bias, allowed, valid, ids, spots, parts):
    heads, count, _ = bias.shape
    extra = SUBLANES if parts > 1 else 0
    width = weights[0].shape[0]
    sds = jax.ShapeDtypeStruct
    return pl.pallas_call(
        functools.partial(layer_kernel, len(packed)),
        out_shape=(sds((1, count), F32),) + (sds((count + extra, width // parts), F32),) * parts,
        in_specs=[VMEM] * (len(packed) + 14),
        out_specs=(VMEM,) * (1 + parts),
        compiler_params=limit(14 if parts > 1 else 40),
        cost_estimate=pl.CostEstimate(
            flops=2_500_000_000, bytes_accessed=8_000_000, transcendentals=400_000
        ),
        name="layer",
    )(spots, *packed, *weights, b_in.reshape(1, -1), bias, allowed, valid, ids)


def pack_kernel(neg_ids, table, out_ref, ids, sems):
    nrows, width = table.shape
    body_copy = pltpu.make_async_copy(table, out_ref.at[pl.ds(0, nrows)], sems.at[0])
    body_copy.start()
    id_copy = pltpu.make_async_copy(neg_ids, ids, sems.at[1])
    id_copy.start()
    id_copy.wait()
    tail = jnp.zeros((1, width - ids.shape[1]), F32)
    row = jnp.concatenate([ids[...].astype(F32), tail], 1)
    out_ref[nrows:] = jnp.broadcast_to(row, (SUBLANES, width))
    body_copy.wait()


def pack(neg_ids, table):
    nrows, width = table.shape
    return pl.pallas_call(
        pack_kernel,
        out_shape=jax.ShapeDtypeStruct((nrows + SUBLANES, width), F32),
        in_specs=[pl.BlockSpec(memory_space=pl.ANY)] * 2,
        out_specs=VMEM,
        scratch_shapes=[pltpu.VMEM(neg_ids.shape, jnp.int32), pltpu.SemaphoreType.DMA((2,))],
        compiler_params=limit(4),
        cost_estimate=pl.CostEstimate(flops=0, bytes_accessed=600_000, transcendentals=0),
        name="pack",
    )(neg_ids, table)


def chosen_rows(owners, names, shards):
    nrows = shards[0].shape[0]
    hot = [names - owner * nrows == lanes((names.shape[0], nrows)) for owner in owners]
    hot = jnp.where(jnp.concatenate(hot, 1), 1.0, 0.0).astype(BF16)
    high, low = halves(jnp.concatenate(shards, 0))
    dot = functools.partial(lax.dot_general, dimension_numbers=NN, preferred_element_type=F32)
    return dot(hot, high) + dot(hot, low)


def fetch_kernel(side, spots, items, partial, panel, *refs):
    *shards, out_ref = refs
    nneg = panel.shape[0]
    nrows = shards[0].shape[0] - SUBLANES
    count = items.shape[1]
    far = nneg * len(shards)
    names = items[count * side : count * (side + 1)]
    if side:
        wanted = [shard[nrows : nrows + 1, :nneg].astype(jnp.int32) for shard in shards]
        names = jnp.concatenate([names, column(jnp.concatenate(wanted, 1))[:far]], 0)
    owners = [spots[step : step + 1] for step in range(1, 1 + len(shards))]
    chosen = chosen_rows(owners, names, [shard[:nrows] for shard in shards])
    out_ref[:count] = partial[count * side : count * (side + 1)] + chosen[:count]
    if side:
        out_ref[count : count + nneg] = panel[...]
        out_ref[count + nneg :] = unit_of(chosen[count:])[0]


def fetch(side, spots, items, partial, panel, shards):
    nneg, width = panel.shape
    count = items.shape[1]
    extra = nneg * (1 + len(shards)) if side else 0
    return pl.pallas_call(
        functools.partial(fetch_kernel, side),
        out_shape=jax.ShapeDtypeStruct((count + extra, width), F32),
        in_specs=[VMEM] * (4 + len(shards)),
        out_specs=VMEM,
        compiler_params=limit(6),
        cost_estimate=pl.CostEstimate(flops=200_000_000, bytes_accessed=2_000_000, transcendentals=0),
        name="fetch",
    )(spots, items, partial, panel, *shards)


def gather_kernel(first, spots, *refs):
    *grads, out_ref = refs
    count = grads[0].shape[0] - SUBLANES
    tokens = [jnp.concatenate(halves(grad[:count]), 1) for grad in grads]
    tokens = jnp.concatenate(tokens, 0)
    names = jnp.concatenate([grad[count : count + 1] for grad in grads], 1).astype(jnp.int32)
    chips, nrows, part = out_ref.shape
    for step in range(chips):
        base = jnp.concatenate([spots[first + step : first + step + 1, :count] * nrows] * len(grads), 1)
        hot = rows((nrows, names.shape[1])) == names - base
        hot = jnp.where(hot, 1.0, 0.0).astype(BF16)
        both = lax.dot_general(hot, tokens, NN, preferred_element_type=F32)
        out_ref[step] = both[:, :part] + both[:, part:]


def gather(first, spots, grads, nrows, chips):
    return pl.pallas_call(
        functools.partial(gather_kernel, first),
        out_shape=jax.ShapeDtypeStruct((chips, nrows, grads[0].shape[1]), F32),
        in_specs=[VMEM] * (1 + len(grads)),
        out_specs=VMEM,
        compiler_params=limit(4),
        cost_estimate=pl.CostEstimate(flops=150_000_000, bytes_accessed=1_000_000, transcendentals=0),
        name="gather",
    )(spots, *grads)


def swap(value, axis, step, size):
    return lax.ppermute(value, axis, [(i, i ^ step) for i in range(size)])


def direct(item_ids, lengths, buckets, neg_ids, table, w_in, b_in, w_out, rab):
    groups = lax.axis_size("group")
    shards = lax.axis_size("shard")
    group = lax.axis_index("group")
    chips = groups // 2
    nrows = table.shape[0]
    own_side = [group ^ (2 * step) for step in range(chips)]
    scalars = own_side + [index ^ 1 for index in own_side] + [lax.axis_index("shard")]
    where = jnp.stack(scalars).astype(jnp.int32)
    item_row = item_ids.reshape(1, -1)
    neg_row = neg_ids.reshape(1, -1)
    packed = pack(neg_row, table)
    panels = [swap(packed, "group", 2 * step, groups) for step in range(1, chips)]
    pair = jnp.concatenate([item_row, swap(item_row, "group", 1, groups)], 0)
    *weights, bias, allowed, valid, items, partial, panel, spots = prepare(
        lengths, w_in, w_out, rab, buckets, (where, pair, neg_row, table)
    )
    other = fetch(1, spots, items, partial, panel, panels)
    mine = fetch(0, spots, items, partial, panel, panels)
    theirs = swap(other, "group", 1, groups)
    loss, *grads = layer(
        theirs,
        other,
        mine,
        weights=weights,
        b_in=b_in,
        bias=bias,
        allowed=allowed,
        valid=valid,
        ids=item_row,
        spots=spots,
        parts=shards,
    )
    blocks = [grads[0]] + [swap(grads[step], "shard", step, shards) for step in range(1, shards)]
    blocks = [blocks[0], *blocks[:0:-1]]
    other = gather(chips, spots, blocks, nrows, chips)
    own = gather(0, spots, blocks, nrows, chips) + swap(other, "group", 1, groups)
    total = own[0]
    for step in (1,3,2):
        total = total + swap(own[step], "group", 2 * step, groups)
    columns = [total] + [swap(total, "shard", step, shards) for step in range(1, shards)]
    plane_row = spots[-1:]
    wide = []
    for spot in range(shards):
        block = columns[0]
        for step in range(1, shards):
            block = jnp.where((plane_row ^ step) == spot, columns[step], block)
        wide.append(block)
    return jnp.concatenate(wide, 1), loss


def picker_of(wanted, rows_dev):
    flat = wanted.reshape(-1)
    return (flat[:, None] == jnp.arange(rows_dev, dtype=jnp.int32)[None, :]).astype(F32)


def by_request(item_ids, lengths, buckets, neg_ids, table, w_in, b_in, w_out, rab):
    high = lax.Precision.HIGHEST
    *weights, bias, allowed, valid = prepare(lengths, w_in, w_out, rab, buckets)
    groups = lax.axis_size("group")
    rows_dev, width = table.shape
    count = item_ids.shape[0]
    capacity = max(2, 2 * count // groups)
    slots = groups * capacity
    owner = item_ids // rows_dev
    member = (owner[:, None] == jnp.arange(groups, dtype=jnp.int32)[None, :]).astype(jnp.int32)
    rank = jnp.sum(member * (jnp.cumsum(member, 0) - 1), 1)
    target_slot = owner * capacity + rank
    requests = (
        jnp.full((slots,), -1, jnp.int32)
        .at[target_slot]
        .set(item_ids % rows_dev)
        .reshape(groups, capacity)
    )
    own_negatives, _ = unit_of(table[neg_ids.reshape(-1) % rows_dev])
    panel_rows = lax.all_gather(own_negatives, "group", axis=0, tiled=True)
    incoming = lax.all_to_all(requests, "group", split_axis=0, concat_axis=0, tiled=True)
    picker = picker_of(incoming, rows_dev)
    served = jnp.dot(picker, table, precision=high).reshape(groups, capacity, width)
    returned = lax.all_to_all(served, "group", split_axis=0, concat_axis=0, tiled=True)
    emb = returned.reshape(slots, width)[target_slot]
    packed = jnp.concatenate([emb, panel_rows], 0)
    loss, d_emb = layer(
        packed,
        weights=weights,
        b_in=b_in,
        bias=bias,
        allowed=allowed,
        valid=valid,
        ids=item_ids.reshape(1, -1),
        spots=jnp.zeros((1, LANES), jnp.int32),
        parts=1,
    )
    outgoing = jnp.zeros((slots, width), F32).at[target_slot].set(d_emb)
    arrived = lax.all_to_all(
        outgoing.reshape(groups, capacity, width), "group", split_axis=0, concat_axis=0, tiled=True
    )
    partial_grad = jnp.dot(picker.T, arrived.reshape(slots, width), precision=high)
    return lax.psum(partial_grad, "shard"), loss


def body(item_ids, seq_lengths, time_buckets, neg_ids, table, w_in, b_in, w_out, rab):
    groups = lax.axis_size("group")
    shards = lax.axis_size("shard")
    width = table.shape[1]
    small = groups in (2, 4, 8, 16) and shards & (shards - 1) == 0 and shards > 1
    small = small and item_ids.shape[0] == LANES and shards * LANES == width
    plan = direct if small else by_request
    grad, loss = plan(
        item_ids, seq_lengths, time_buckets, neg_ids, table, w_in, b_in, w_out, rab
    )
    return grad, loss.reshape(-1)


def solution(mesh):
    in_specs = (
        P(("shard", "group")),
        P(("shard", "group"), None),
        P(("shard", "group")),
        P("shard", "group"),
        P("group", None),
        P(),
        P(),
        P(),
        P(),
    )
    out_specs = (P("group", None), P(("shard", "group")))
    return jax.shard_map(body, mesh=mesh, in_specs=in_specs, out_specs=out_specs, check_vma=False)
```

```python
import functools

import jax
import jax.numpy as jnp
from jax import lax
from jax.experimental import pallas as pl
from jax.experimental.pallas import tpu as pltpu
from jax.sharding import PartitionSpec as P

MOST_LEN = 64
TEMPER = 0.05
LANES = 128
SUBLANES = 8
F32 = jnp.float32
BF16 = jnp.bfloat16
NN = (((1,), (0,)), ((), ()))
NT = (((1,), (1,)), ((), ()))
TN = (((0,), (0,)), ((), ()))
VMEM = pl.BlockSpec(memory_space=pltpu.VMEM)
SMEM = pl.BlockSpec(memory_space=pltpu.SMEM)


def limit(mebibytes):
    return pltpu.CompilerParams(vmem_limit_bytes=mebibytes * 1024 * 1024)


def halves(value):
    high = value.astype(BF16)
    return high, (value - high.astype(F32)).astype(BF16)


def mul(left, right, dims=NN):
    lh, ll = left
    rh, rl = right
    dot = functools.partial(lax.dot_general, dimension_numbers=dims, preferred_element_type=F32)
    both = dot(jnp.concatenate([lh, ll], 0), rh)
    count = lh.shape[0]
    return both[:count] + (both[count:] + dot(lh, rl))


def mul_small(left, right, dims=NN):
    lh, ll = left
    rh, rl = right
    if dims == NN:
        wide = jnp.concatenate([rh, rl], 1)
        right = jnp.concatenate([wide, wide], 0)
    else:
        right = jnp.concatenate([jnp.concatenate([rh, rh], 1), jnp.concatenate([rl, rl], 1)], 0)
    both = lax.dot_general(jnp.concatenate([lh, ll], 1), right, dims, preferred_element_type=F32)
    half = both.shape[1] // 2
    return both[:, :half] + both[:, half:]


def sum_last(value):
    return jnp.sum(value, axis=-1, keepdims=True)


def mean_last(value):
    return jnp.mean(value, axis=-1, keepdims=True)


def lanes(shape):
    return lax.broadcasted_iota(jnp.int32, shape, 1)


def rows(shape):
    return lax.broadcasted_iota(jnp.int32, shape, 0)


def spread(row, count):
    wide = jnp.broadcast_to(row.astype(F32), (count, count))
    return wide.T.astype(jnp.int32)


def column(row):
    short = LANES - row.shape[1]
    if short:
        row = jnp.concatenate([row, jnp.full((1, short), -1, jnp.int32)], 1)
    return spread(row, LANES)


def norm_of(value):
    centered = value - mean_last(value)
    scale = lax.rsqrt(mean_last(centered * centered) + 1e-05)
    return centered * scale, scale


def norm_back(grad, normed, scale):
    return scale * (grad - mean_last(grad) - normed * mean_last(grad * normed))


def unit_of(value):
    scale = lax.rsqrt(sum_last(value * value) + 1e-06)
    return value * scale, scale


def unit_back(grad, united, scale):
    return scale * (grad - united * sum_last(grad * united))


def time_bias(rab, buckets, bias):
    count = buckets.shape[1]
    gap = jnp.abs(buckets - spread(buckets, count))
    heads, nbuck = rab.shape
    for head in range(heads):
        level = jnp.concatenate([rab[head : head + 1, :], jnp.zeros((1, LANES - nbuck), F32)], 1)
        level = jnp.broadcast_to(level, (count, LANES))
        bias[head] = jnp.take_along_axis(level, gap, axis=1)


def masks(lengths, number):
    square = (LANES, LANES)
    place_i, place_j = rows(square), lanes(square)
    upto = jnp.where(place_i <= place_j, spread(lengths, LANES), 0)
    ends = spread(jnp.sum(upto, axis=0, keepdims=True), LANES)
    real = place_i < number
    seg = jnp.sum((real & (place_j >= ends)).astype(jnp.int32), axis=0, keepdims=True)
    following = jnp.sum((real & (place_j + 1 >= ends)).astype(jnp.int32), axis=0, keepdims=True)
    near = (seg == following) & (lanes((1, LANES)) + 1 < LANES)
    allowed = (place_j <= place_i) & (spread(seg, LANES) == seg)
    valid = spread(near.astype(jnp.int32), LANES)
    return jnp.where(allowed, 1.0 / MOST_LEN, 0.0).astype(F32), valid.astype(F32)


def prepare_kernel(
    number, small, w_in, w_out, rab, in_h, in_l, in_th, in_tl, out_h, out_l, out_th, out_tl, bias, allowed, valid
):
    width, hidden = w_in.shape
    allowed[...], valid[...] = masks(small[2:3], number)
    high, low = halves(w_out[...])
    out_h[...], out_l[...] = high, low
    out_th[...], out_tl[...] = high.T, low.T
    for start in range(0, hidden, width):
        span = slice(start, start + width)
        high, low = halves(w_in[:, span])
        in_h[:, span], in_l[:, span] = high, low
        in_th[span, :], in_tl[span, :] = high.T, low.T
    time_bias(rab, small[1:2], bias)


def prepare_own_kernel(number, nneg, where, small, w_in, w_out, rab, other_ids, table, *outs):
    *weights, items, found, panel, spots = outs
    for index in range(where.shape[0]):
        spots[index : index + 1, :] = jnp.full((1, LANES), where[index], jnp.int32)
    prepare_kernel(number, small, w_in, w_out, rab, *weights)
    count = other_ids.shape[1]
    me, other = spread(small[0:1], count), spread(other_ids[...], count)
    items[:count] = me
    items[count:] = other
    names = jnp.concatenate([me, other, spread(small[3:4], LANES)[:nneg]], 0)
    chosen = chosen_rows([where[0]], names, [table[...]])
    found[...] = chosen[: 2 * count]
    panel[...] = unit_of(chosen[2 * count :])[0]


def small_rows(*values):
    values = [value.reshape(-1) for value in values]
    return jnp.stack([jnp.pad(value, (0, LANES - value.size)) for value in values])


def prepare(small, number, w_in, w_out, rab, where=None, other_ids=None, table=None, nneg=0):
    count = small.shape[1]
    width, hidden = w_in.shape
    heads = rab.shape[0]
    sds = jax.ShapeDtypeStruct
    outs = (
        *(sds((width, hidden), BF16),) * 2,
        *(sds((hidden, width), BF16),) * 2,
        *(sds((width, width), BF16),) * 4,
        sds((heads, count, count), F32),
        *(sds((count, count), F32),) * 2,
    )
    kernel, args, specs = functools.partial(prepare_kernel, number), (small, w_in, w_out, rab), []
    if where is not None:
        kernel, specs = functools.partial(prepare_own_kernel, number, nneg), [SMEM]
        args = (where, *args, other_ids, table)
        outs += (
            sds((2 * count, count), jnp.int32),
            sds((2 * count, width), F32),
            sds((nneg, width), F32),
            sds((where.shape[0], LANES), jnp.int32),
        )
    return pl.pallas_call(
        kernel,
        out_shape=outs,
        in_specs=specs + [VMEM] * (len(args) - len(specs)),
        out_specs=(VMEM,) * len(outs),
        compiler_params=limit(12),
        cost_estimate=pl.CostEstimate(flops=200_000_000, bytes_accessed=12_000_000, transcendentals=0),
        name="prepare",
    )(*args)


def layer_kernel(pieces, spots, *refs):
    packed = refs[:pieces]
    in_h, in_l, in_th, in_tl, out_h, out_l, out_th, out_tl = refs[pieces : pieces + 8]
    b_in, bias, allowed_ref, valid_ref, ids = refs[pieces + 8 : pieces + 13]
    loss_ref = refs[pieces + 13]
    grads = refs[pieces + 14 :]
    heads, count, _ = bias.shape
    width = in_h.shape[0]
    each = width // heads
    emb = packed[0][:count]
    if pieces > 1:
        emb = emb + packed[2][...]
    allowed = allowed_ref[...]
    valid = valid_ref[:, :1]
    square = (count, count)
    place_i, place_j = rows(square), lanes(square)
    xn, x_scale = norm_of(emb)
    w_out = (out_h[...], out_l[...])
    xn_parts = halves(xn)
    hidden, slope = {}, {}
    for part in (2, 3, 1, 0):
        span = slice(width * part, width * (part + 1))
        pre = mul(xn_parts, (in_h[:, span], in_l[:, span])) + b_in[:, span]
        sig = jax.nn.sigmoid(pre)
        hidden[part] = pre * sig
        slope[part] = sig * (1.0 + pre * (1.0 - sig))
    upart = hidden[0]
    kept = []
    mixed = []
    for head in range(heads):
        vh, qh, kh = (
            halves(hidden[part][:, each * head : each * (head + 1)])
            for part in (1, 2, 3)
        )
        score = mul_small(qh, kh, NT) * each ** (-0.5) + bias[head]
        gate = jax.nn.sigmoid(score)
        weight = score * gate * allowed
        bend = gate * (1.0 + score * (1.0 - gate)) * allowed
        mixed.append(mul_small(halves(weight), vh))
        kept.append((vh, qh, kh, halves(weight.T), bend))
    yn, y_scale = norm_of(jnp.concatenate(mixed, axis=1))
    out = mul(halves(yn * upart), w_out) + emb
    states, s_scale = unit_of(out)
    united, e_scale = unit_of(emb)
    last = rows((count, width)) == count - 1
    target = jnp.where(last, 0.0, pltpu.roll(united, count - 1, 0))
    positive = sum_last(states * target) * (1.0 / TEMPER)
    expos = jnp.exp(positive)
    state_parts = halves(states)
    panel = halves(jnp.concatenate([piece[count:] for piece in packed[:2]], 0))
    exps = jnp.exp(mul(state_parts, panel, NT) * (1.0 / TEMPER))
    zneg = sum_last(exps)
    pulled = mul(halves(exps), panel)
    total = expos + zneg
    loss = valid * (jnp.log(total) - positive)
    loss_ref[...] = jnp.sum(jnp.where(place_i == place_j, loss, 0.0), axis=0, keepdims=True)
    share = valid * (expos / total - 1.0) * (1.0 / TEMPER)
    d_states = share * target + pulled * (valid / total * (1.0 / TEMPER))
    d_out = unit_back(d_states, states, s_scale)
    first = rows((count, width)) == 0
    d_next = jnp.where(first, 0.0, pltpu.roll(share * states, 1, 0))
    d_emb = d_out + unit_back(d_next, united, e_scale)
    d_gated = mul(halves(d_out), (out_th[...], out_tl[...]))
    d_mixed = norm_back(d_gated * upart, yn, y_scale)

    def input_grad(part, grad):
        span = slice(width * part, width * (part + 1))
        return mul(halves(grad * slope[part]), (in_th[span], in_tl[span]))

    d_xn = input_grad(0, d_gated * yn)
    d_v, d_q, d_k = [], [], []
    for head in range(heads):
        vh, qh, kh, weight_t, bend = kept[head]
        d_mh = halves(d_mixed[:, each * head : each * (head + 1)])
        d_v.append(mul_small(weight_t, d_mh))
        d_score = mul_small(d_mh, vh, NT) * bend * each ** (-0.5)
        d_q.append(mul_small(halves(d_score), kh))
        d_k.append(mul_small(halves(d_score.T), qh))
    for part, grad in ((1, d_v), (2, d_q), (3, d_k)):
        d_xn = d_xn + input_grad(part, jnp.concatenate(grad, axis=1))
    d_emb = d_emb + norm_back(d_xn, xn, x_scale)
    if len(grads) == 1:
        grads[0][...] = d_emb
        return
    part = width // len(grads)
    plane = spots[spots.shape[0] - 1 :, :part]
    for step, out_ref in enumerate(grads):
        block = d_emb[:, :part]
        for spot in range(1, len(grads)):
            mine = (plane ^ step) == spot
            block = jnp.where(mine, d_emb[:, part * spot : part * (spot + 1)], block)
        out_ref[:count] = block
        out_ref[count:] = jnp.broadcast_to(ids[...].astype(F32), (SUBLANES, part))


def layer(*packed, weights, b_in, bias, allowed, valid, ids, spots, parts):
    heads, count, _ = bias.shape
    extra = SUBLANES if parts > 1 else 0
    width = weights[0].shape[0]
    sds = jax.ShapeDtypeStruct
    return pl.pallas_call(
        functools.partial(layer_kernel, len(packed)),
        out_shape=(sds((1, count), F32),) + (sds((count + extra, width // parts), F32),) * parts,
        in_specs=[VMEM] * (len(packed) + 14),
        out_specs=(VMEM,) * (1 + parts),
        compiler_params=limit(14 if parts > 1 else 40),
        cost_estimate=pl.CostEstimate(
            flops=2_500_000_000, bytes_accessed=8_000_000, transcendentals=400_000
        ),
        name="layer",
    )(spots, *packed, *weights, b_in.reshape(1, -1), bias, allowed, valid, ids)


def pack(neg_ids, table):
    nrows, width = table.shape
    body = lax.pad(table, jnp.float32(0), [(0, SUBLANES, 0), (0, 0, 0)])
    tile = [(nrows, SUBLANES - 1, 0), (0, width - neg_ids.shape[1], 0)]
    return body + lax.pad(neg_ids, jnp.int32(0), tile).astype(F32)


def chosen_rows(owners, names, shards):
    nrows = shards[0].shape[0]
    hot = [names - owner * nrows == lanes((names.shape[0], nrows)) for owner in owners]
    hot = jnp.where(jnp.concatenate(hot, 1), 1.0, 0.0).astype(BF16)
    high, low = halves(jnp.concatenate(shards, 0))
    dot = functools.partial(lax.dot_general, dimension_numbers=NN, preferred_element_type=F32)
    return dot(hot, high) + dot(hot, low)


def fetch_kernel(side, spots, items, partial, panel, *refs):
    *shards, out_ref = refs
    nneg = panel.shape[0]
    nrows = shards[0].shape[0] - SUBLANES
    count = items.shape[1]
    far = nneg * len(shards)
    names = items[count * side : count * (side + 1)]
    if side:
        wanted = [shard[nrows : nrows + 1, :nneg].astype(jnp.int32) for shard in shards]
        names = jnp.concatenate([names, column(jnp.concatenate(wanted, 1))[:far]], 0)
    owners = [spots[step : step + 1] for step in range(1, 1 + len(shards))]
    chosen = chosen_rows(owners, names, [shard[:nrows] for shard in shards])
    out_ref[:count] = partial[count * side : count * (side + 1)] + chosen[:count]
    if side:
        out_ref[count : count + nneg] = panel[...]
        out_ref[count + nneg :] = unit_of(chosen[count:])[0]


def fetch(side, spots, items, partial, panel, shards):
    nneg, width = panel.shape
    count = items.shape[1]
    extra = nneg * (1 + len(shards)) if side else 0
    return pl.pallas_call(
        functools.partial(fetch_kernel, side),
        out_shape=jax.ShapeDtypeStruct((count + extra, width), F32),
        in_specs=[VMEM] * (4 + len(shards)),
        out_specs=VMEM,
        compiler_params=limit(6),
        cost_estimate=pl.CostEstimate(flops=200_000_000, bytes_accessed=2_000_000, transcendentals=0),
        name="fetch",
    )(spots, items, partial, panel, *shards)


def gather_kernel(first, spots, *refs):
    *grads, out_ref = refs
    count = grads[0].shape[0] - SUBLANES
    tokens = [jnp.concatenate(halves(grad[:count]), 1) for grad in grads]
    tokens = jnp.concatenate(tokens, 0)
    names = jnp.concatenate([grad[count : count + 1] for grad in grads], 1).astype(jnp.int32)
    chips, nrows, part = out_ref.shape
    for step in range(chips):
        base = jnp.concatenate([spots[first + step : first + step + 1, :count] * nrows] * len(grads), 1)
        hot = rows((nrows, names.shape[1])) == names - base
        hot = jnp.where(hot, 1.0, 0.0).astype(BF16)
        both = lax.dot_general(hot, tokens, NN, preferred_element_type=F32)
        out_ref[step] = both[:, :part] + both[:, part:]


def gather(first, spots, grads, nrows, chips):
    return pl.pallas_call(
        functools.partial(gather_kernel, first),
        out_shape=jax.ShapeDtypeStruct((chips, nrows, grads[0].shape[1]), F32),
        in_specs=[VMEM] * (1 + len(grads)),
        out_specs=VMEM,
        compiler_params=limit(4),
        cost_estimate=pl.CostEstimate(flops=150_000_000, bytes_accessed=1_000_000, transcendentals=0),
        name="gather",
    )(spots, *grads)


def swap(value, axis, step, size):
    return lax.ppermute(value, axis, [(i, i ^ step) for i in range(size)])


def direct(item_ids, lengths, buckets, neg_ids, table, w_in, b_in, w_out, rab):
    groups = lax.axis_size("group")
    shards = lax.axis_size("shard")
    group = lax.axis_index("group")
    chips = groups // 2
    nrows = table.shape[0]
    own_side = [group ^ (2 * step) for step in range(chips)]
    scalars = own_side + [index ^ 1 for index in own_side] + [lax.axis_index("shard")]
    where = jnp.stack(scalars).astype(jnp.int32)
    item_row = item_ids.reshape(1, -1)
    neg_row = neg_ids.reshape(1, -1)
    packed = pack(neg_row, table)
    panels = [swap(packed, "group", 2 * step, groups) for step in range(1, chips)]
    other_ids = swap(item_row, "group", 1, groups)
    small = small_rows(item_ids, buckets, lengths, neg_ids)
    *weights, bias, allowed, valid, items, partial, panel, spots = prepare(
        small, lengths.size, w_in, w_out, rab, where, other_ids, table, neg_ids.size
    )
    other = fetch(1, spots, items, partial, panel, panels)
    mine = fetch(0, spots, items, partial, panel, panels)
    theirs = swap(other, "group", 1, groups)
    loss, *grads = layer(
        theirs,
        other,
        mine,
        weights=weights,
        b_in=b_in,
        bias=bias,
        allowed=allowed,
        valid=valid,
        ids=small[:1],
        spots=spots,
        parts=shards,
    )
    blocks = [grads[0]] + [swap(grads[step], "shard", step, shards) for step in range(1, shards)]
    blocks = [blocks[0], *blocks[:0:-1]]
    other = gather(chips, spots, blocks, nrows, chips)
    own = gather(0, spots, blocks, nrows, chips) + swap(other, "group", 1, groups)
    total = own[0]
    for step in (1,3,2):
        total = total + swap(own[step], "group", 2 * step, groups)
    columns = [total] + [swap(total, "shard", step, shards) for step in range(1, shards)]
    plane_row = spots[-1:]
    wide = []
    for spot in range(shards):
        block = columns[0]
        for step in range(1, shards):
            block = jnp.where((plane_row ^ step) == spot, columns[step], block)
        wide.append(block)
    return jnp.concatenate(wide, 1), loss


def picker_of(wanted, rows_dev):
    flat = wanted.reshape(-1)
    return (flat[:, None] == jnp.arange(rows_dev, dtype=jnp.int32)[None, :]).astype(F32)


def by_request(item_ids, lengths, buckets, neg_ids, table, w_in, b_in, w_out, rab):
    high = lax.Precision.HIGHEST
    small = small_rows(item_ids, buckets, lengths, neg_ids)
    *weights, bias, allowed, valid = prepare(small, lengths.size, w_in, w_out, rab)
    groups = lax.axis_size("group")
    rows_dev, width = table.shape
    count = item_ids.shape[0]
    capacity = max(2, 2 * count // groups)
    slots = groups * capacity
    owner = item_ids // rows_dev
    member = (owner[:, None] == jnp.arange(groups, dtype=jnp.int32)[None, :]).astype(jnp.int32)
    rank = jnp.sum(member * (jnp.cumsum(member, 0) - 1), 1)
    target_slot = owner * capacity + rank
    requests = (
        jnp.full((slots,), -1, jnp.int32)
        .at[target_slot]
        .set(item_ids % rows_dev)
        .reshape(groups, capacity)
    )
    own_negatives, _ = unit_of(table[neg_ids.reshape(-1) % rows_dev])
    panel_rows = lax.all_gather(own_negatives, "group", axis=0, tiled=True)
    incoming = lax.all_to_all(requests, "group", split_axis=0, concat_axis=0, tiled=True)
    picker = picker_of(incoming, rows_dev)
    served = jnp.dot(picker, table, precision=high).reshape(groups, capacity, width)
    returned = lax.all_to_all(served, "group", split_axis=0, concat_axis=0, tiled=True)
    emb = returned.reshape(slots, width)[target_slot]
    packed = jnp.concatenate([emb, panel_rows], 0)
    loss, d_emb = layer(
        packed,
        weights=weights,
        b_in=b_in,
        bias=bias,
        allowed=allowed,
        valid=valid,
        ids=small[:1],
        spots=jnp.zeros((1, LANES), jnp.int32),
        parts=1,
    )
    outgoing = jnp.zeros((slots, width), F32).at[target_slot].set(d_emb)
    arrived = lax.all_to_all(
        outgoing.reshape(groups, capacity, width), "group", split_axis=0, concat_axis=0, tiled=True
    )
    partial_grad = jnp.dot(picker.T, arrived.reshape(slots, width), precision=high)
    return lax.psum(partial_grad, "shard"), loss


def body(item_ids, seq_lengths, time_buckets, neg_ids, table, w_in, b_in, w_out, rab):
    groups = lax.axis_size("group")
    shards = lax.axis_size("shard")
    width = table.shape[1]
    small = groups in (2, 4, 8, 16) and shards & (shards - 1) == 0 and shards > 1
    small = small and item_ids.shape[0] == LANES and shards * LANES == width
    plan = direct if small else by_request
    grad, loss = plan(
        item_ids, seq_lengths, time_buckets, neg_ids, table, w_in, b_in, w_out, rab
    )
    return grad, loss.reshape(-1)


def solution(mesh):
    in_specs = (
        P(("shard", "group")),
        P(("shard", "group"), None),
        P(("shard", "group")),
        P("shard", "group"),
        P("group", None),
        P(),
        P(),
        P(),
        P(),
    )
    out_specs = (P("group", None), P(("shard", "group")))
    return jax.shard_map(body, mesh=mesh, in_specs=in_specs, out_specs=out_specs, check_vma=False)
```

```python
import functools

import jax
import jax.numpy as jnp
from jax import lax
from jax.experimental import pallas as pl
from jax.experimental.pallas import tpu as pltpu
from jax.sharding import PartitionSpec as P

MOST_LEN = 64
TEMPER = 0.05
LANES = 128
SUBLANES = 8
F32 = jnp.float32
BF16 = jnp.bfloat16
NN = (((1,), (0,)), ((), ()))
NT = (((1,), (1,)), ((), ()))
TN = (((0,), (0,)), ((), ()))
VMEM = pl.BlockSpec(memory_space=pltpu.VMEM)
SMEM = pl.BlockSpec(memory_space=pltpu.SMEM)


def limit(mebibytes):
    return pltpu.CompilerParams(vmem_limit_bytes=mebibytes * 1024 * 1024)


def halves(value):
    high = value.astype(BF16)
    return high, (value - high.astype(F32)).astype(BF16)


def mul(left, right, dims=NN):
    lh, ll = left
    rh, rl = right
    dot = functools.partial(lax.dot_general, dimension_numbers=dims, preferred_element_type=F32)
    both = dot(jnp.concatenate([lh, ll], 0), rh)
    count = lh.shape[0]
    return both[:count] + (both[count:] + dot(lh, rl))


def mul_small(left, right, dims=NN):
    lh, ll = left
    rh, rl = right
    if dims == NN:
        wide = jnp.concatenate([rh, rl], 1)
        right = jnp.concatenate([wide, wide], 0)
    else:
        right = jnp.concatenate([jnp.concatenate([rh, rh], 1), jnp.concatenate([rl, rl], 1)], 0)
    both = lax.dot_general(jnp.concatenate([lh, ll], 1), right, dims, preferred_element_type=F32)
    half = both.shape[1] // 2
    return both[:, :half] + both[:, half:]


def sum_last(value):
    return jnp.sum(value, axis=-1, keepdims=True)


def mean_last(value):
    return jnp.mean(value, axis=-1, keepdims=True)


def lanes(shape):
    return lax.broadcasted_iota(jnp.int32, shape, 1)


def rows(shape):
    return lax.broadcasted_iota(jnp.int32, shape, 0)


def spread(row, count):
    wide = jnp.broadcast_to(row.astype(F32), (count, count))
    return wide.T.astype(jnp.int32)


def column(row):
    short = LANES - row.shape[1]
    if short:
        row = jnp.concatenate([row, jnp.full((1, short), -1, jnp.int32)], 1)
    return spread(row, LANES)


def norm_of(value):
    centered = value - mean_last(value)
    scale = lax.rsqrt(mean_last(centered * centered) + 1e-05)
    return centered * scale, scale


def norm_back(grad, normed, scale):
    return scale * (grad - mean_last(grad) - normed * mean_last(grad * normed))


def unit_of(value):
    scale = lax.rsqrt(sum_last(value * value) + 1e-06)
    return value * scale, scale


def unit_back(grad, united, scale):
    return scale * (grad - united * sum_last(grad * united))


def time_bias(rab, buckets, bias):
    count = buckets.shape[1]
    gap = jnp.abs(buckets - spread(buckets, count))
    heads, nbuck = rab.shape
    for head in range(heads):
        level = jnp.concatenate([rab[head : head + 1, :], jnp.zeros((1, LANES - nbuck), F32)], 1)
        level = jnp.broadcast_to(level, (count, LANES))
        bias[head] = jnp.take_along_axis(level, gap, axis=1)


def masks(lengths, number):
    square = (LANES, LANES)
    place_i, place_j = rows(square), lanes(square)
    upto = jnp.where(place_i <= place_j, spread(lengths, LANES), 0)
    ends = spread(jnp.sum(upto, axis=0, keepdims=True), LANES)
    real = place_i < number
    seg = jnp.sum((real & (place_j >= ends)).astype(jnp.int32), axis=0, keepdims=True)
    following = jnp.sum((real & (place_j + 1 >= ends)).astype(jnp.int32), axis=0, keepdims=True)
    near = (seg == following) & (lanes((1, LANES)) + 1 < LANES)
    allowed = (place_j <= place_i) & (spread(seg, LANES) == seg)
    valid = spread(near.astype(jnp.int32), LANES)
    return jnp.where(allowed, 1.0 / MOST_LEN, 0.0).astype(F32), valid.astype(F32)


def weights_kernel(w_in, w_out, after, in_h, in_l, in_th, in_tl, out_h, out_l, out_th, out_tl, zeros):
    width, hidden = w_in.shape
    zeros[...] = jnp.zeros(zeros.shape, jnp.int32)
    high, low = halves(w_out[...])
    out_h[...], out_l[...] = high, low
    out_th[...], out_tl[...] = high.T, low.T
    for start in range(0, hidden, width):
        span = slice(start, start + width)
        high, low = halves(w_in[:, span])
        in_h[:, span], in_l[:, span] = high, low
        in_th[span, :], in_tl[span, :] = high.T, low.T


def weight_halves(w_in, w_out, after):
    width, hidden = w_in.shape
    shapes = [(width, hidden)] * 2 + [(hidden, width)] * 2 + [(width, width)] * 4
    return pl.pallas_call(
        weights_kernel,
        out_shape=(
            *(jax.ShapeDtypeStruct(shape, BF16) for shape in shapes),
            jax.ShapeDtypeStruct((1, LANES), jnp.int32),
        ),
        in_specs=[VMEM] * 2 + [pl.BlockSpec(memory_space=pl.ANY)],
        out_specs=(VMEM,) * 9,
        compiler_params=limit(8),
        cost_estimate=pl.CostEstimate(flops=4_000_000, bytes_accessed=15_000_000, transcendentals=0),
        name="weight_halves",
    )(w_in, w_out, after)


def prepare_kernel(number, small, rab, bias, allowed, valid):
    allowed[...], valid[...] = masks(small[2:3], number)
    time_bias(rab, small[1:2], bias)


def prepare_own_kernel(number, nneg, where, small, rab, other_ids, shard, *outs):
    *pairs, items, found, panel, spots, zeros = outs
    zeros[...] = jnp.zeros(zeros.shape, F32)
    for index in range(where.shape[0]):
        spots[index : index + 1, :] = jnp.full((1, LANES), where[index], jnp.int32)
    prepare_kernel(number, small, rab, *pairs)
    count = other_ids.shape[1]
    me, other = spread(small[0:1], count), spread(other_ids[...], count)
    items[:count] = me
    items[count:] = other
    names = jnp.concatenate([me, other, spread(small[3:4], LANES)[:nneg]], 0)
    chosen = chosen_rows(names, [(where[0], None, shard[...])])
    found[...] = chosen[: 2 * count]
    panel[...] = unit_of(chosen[2 * count :])[0]


def small_rows(*values):
    total = 0
    for row, value in enumerate(values):
        spots = [(row, len(values) - 1 - row, 0), (0, LANES - value.size, 0)]
        total = total + lax.pad(value.reshape(1, -1), jnp.int32(0), spots)
    return total


def prepare(small, number, rab, where=None, other_ids=None, shard=None, nneg=0):
    count = small.shape[1]
    heads = rab.shape[0]
    sds = jax.ShapeDtypeStruct
    outs = (sds((heads, count, count), F32), *(sds((count, count), F32),) * 2)
    kernel, args, specs = functools.partial(prepare_kernel, number), (small, rab), []
    if where is not None:
        kernel, specs = functools.partial(prepare_own_kernel, number, nneg), [SMEM]
        args = (where, *args, other_ids, shard)
        width = shard.shape[1]
        outs += (
            sds((2 * count, count), jnp.int32),
            sds((2 * count, width), F32),
            sds((nneg, width), F32),
            sds((where.shape[0], LANES), jnp.int32),
            sds((1, width), F32),
        )
    return pl.pallas_call(
        kernel,
        out_shape=outs,
        in_specs=specs + [VMEM] * (len(args) - len(specs)),
        out_specs=(VMEM,) * len(outs),
        compiler_params=limit(6),
        cost_estimate=pl.CostEstimate(flops=200_000_000, bytes_accessed=2_000_000, transcendentals=0),
        name="prepare",
    )(*args)


def layer_kernel(pieces, spots, *refs):
    packed = refs[:pieces]
    in_h, in_l, in_th, in_tl, out_h, out_l, out_th, out_tl = refs[pieces : pieces + 8]
    b_in, bias, allowed_ref, valid_ref, ids = refs[pieces + 8 : pieces + 13]
    loss_ref = refs[pieces + 13]
    grads = refs[pieces + 14 :]
    heads, count, _ = bias.shape
    width = in_h.shape[0]
    each = width // heads
    emb = packed[0][:count]
    if pieces > 1:
        emb = emb + packed[2][...]
    allowed = allowed_ref[...]
    valid = valid_ref[:, :1]
    square = (count, count)
    place_i, place_j = rows(square), lanes(square)
    xn, x_scale = norm_of(emb)
    w_out = (out_h[...], out_l[...])
    xn_parts = halves(xn)
    hidden, slope = {}, {}
    for part in (2, 3, 1, 0):
        span = slice(width * part, width * (part + 1))
        pre = mul(xn_parts, (in_h[:, span], in_l[:, span])) + b_in[:, span]
        sig = jax.nn.sigmoid(pre)
        hidden[part] = pre * sig
        slope[part] = sig * (1.0 + pre * (1.0 - sig))
    upart = hidden[0]
    kept = []
    mixed = []
    for head in range(heads):
        vh, qh, kh = (
            halves(hidden[part][:, each * head : each * (head + 1)])
            for part in (1, 2, 3)
        )
        score = mul_small(qh, kh, NT) * each ** (-0.5) + bias[head]
        gate = jax.nn.sigmoid(score)
        weight = score * gate * allowed
        bend = gate * (1.0 + score * (1.0 - gate)) * allowed
        mixed.append(mul_small(halves(weight), vh))
        kept.append((vh, qh, kh, halves(weight.T), bend))
    yn, y_scale = norm_of(jnp.concatenate(mixed, axis=1))
    out = mul(halves(yn * upart), w_out) + emb
    states, s_scale = unit_of(out)
    united, e_scale = unit_of(emb)
    last = rows((count, width)) == count - 1
    target = jnp.where(last, 0.0, pltpu.roll(united, count - 1, 0))
    positive = sum_last(states * target) * (1.0 / TEMPER)
    expos = jnp.exp(positive)
    state_parts = halves(states)
    panel = halves(jnp.concatenate([piece[count:] for piece in packed[:2]], 0))
    exps = jnp.exp(mul(state_parts, panel, NT) * (1.0 / TEMPER))
    zneg = sum_last(exps)
    pulled = mul(halves(exps), panel)
    total = expos + zneg
    loss = valid * (jnp.log(total) - positive)
    loss_ref[...] = jnp.sum(jnp.where(place_i == place_j, loss, 0.0), axis=0, keepdims=True)
    share = valid * (expos / total - 1.0) * (1.0 / TEMPER)
    d_states = share * target + pulled * (valid / total * (1.0 / TEMPER))
    d_out = unit_back(d_states, states, s_scale)
    first = rows((count, width)) == 0
    d_next = jnp.where(first, 0.0, pltpu.roll(share * states, 1, 0))
    d_emb = d_out + unit_back(d_next, united, e_scale)
    d_gated = mul(halves(d_out), (out_th[...], out_tl[...]))
    d_mixed = norm_back(d_gated * upart, yn, y_scale)

    def input_grad(part, grad):
        span = slice(width * part, width * (part + 1))
        return mul(halves(grad * slope[part]), (in_th[span], in_tl[span]))

    d_xn = input_grad(0, d_gated * yn)
    d_v, d_q, d_k = [], [], []
    for head in range(heads):
        vh, qh, kh, weight_t, bend = kept[head]
        d_mh = halves(d_mixed[:, each * head : each * (head + 1)])
        d_v.append(mul_small(weight_t, d_mh))
        d_score = mul_small(d_mh, vh, NT) * bend * each ** (-0.5)
        d_q.append(mul_small(halves(d_score), kh))
        d_k.append(mul_small(halves(d_score.T), qh))
    for part, grad in ((1, d_v), (2, d_q), (3, d_k)):
        d_xn = d_xn + input_grad(part, jnp.concatenate(grad, axis=1))
    d_emb = d_emb + norm_back(d_xn, xn, x_scale)
    if len(grads) == 1:
        grads[0][...] = d_emb
        return
    part = width // len(grads)
    plane = spots[spots.shape[0] - 1 :, :part]
    for step, out_ref in enumerate(grads):
        block = d_emb[:, :part]
        for spot in range(1, len(grads)):
            mine = (plane ^ step) == spot
            block = jnp.where(mine, d_emb[:, part * spot : part * (spot + 1)], block)
        out_ref[:count] = block
        out_ref[count:] = jnp.broadcast_to(ids[...].astype(F32), (SUBLANES, part))


def layer(*packed, weights, b_in, bias, allowed, valid, ids, spots, parts):
    heads, count, _ = bias.shape
    extra = SUBLANES if parts > 1 else 0
    width = weights[0].shape[0]
    sds = jax.ShapeDtypeStruct
    return pl.pallas_call(
        functools.partial(layer_kernel, len(packed)),
        out_shape=(sds((1, count), F32),) + (sds((count + extra, width // parts), F32),) * parts,
        in_specs=[VMEM] * (len(packed) + 14),
        out_specs=(VMEM,) * (1 + parts),
        compiler_params=limit(14 if parts > 1 else 40),
        cost_estimate=pl.CostEstimate(
            flops=2_500_000_000, bytes_accessed=8_000_000, transcendentals=400_000
        ),
        name="layer",
    )(spots, *packed, *weights, b_in.reshape(1, -1), bias, allowed, valid, ids)


def pack(neg_ids, table):
    nrows, width = table.shape
    body = lax.pad(table, jnp.float32(0), [(0, SUBLANES, 0), (0, 0, 0)])
    tile = [(nrows, SUBLANES - 1, 0), (0, width - neg_ids.shape[1], 0)]
    return body + lax.pad(neg_ids, jnp.int32(0), tile).astype(F32)


def chosen_rows(names, pieces):
    place = jnp.full(names.shape, -1, jnp.int32)
    offset = 0
    for owner, part, held in pieces:
        nrows = held.shape[0] - SUBLANES
        if part is None:
            spot = names - owner * nrows
        else:
            spot = names - (owner * 2 + part) * nrows
        place = jnp.where((spot >= 0) & (spot < nrows), spot + offset, place)
        offset += held.shape[0]
    rest = -offset % LANES
    held = [piece[2] for piece in pieces]
    if rest:
        held.append(jnp.zeros((rest, held[0].shape[1]), F32))
    column = lanes(names.shape)
    hot = [place == column + start for start in range(0, offset + rest, LANES)]
    hot = jnp.where(jnp.concatenate(hot, 1), 1.0, 0.0).astype(BF16)
    high, low = halves(jnp.concatenate(held, 0))
    dot = functools.partial(lax.dot_general, dimension_numbers=NN, preferred_element_type=F32)
    return dot(hot, high) + dot(hot, low)


def fetch_kernel(side, plan, spots, items, partial, panel, *refs):
    *shards, out_ref = refs
    nneg = panel.shape[0]
    count = items.shape[1]
    odd = spots[spots.shape[0] - 1 :, :] & 1
    pieces, wanted = [], []
    for (step, kind), shard in zip(plan, shards):
        nrows = shard.shape[0] - SUBLANES
        part = {0: None, 1: odd, 2: 1 - odd}[kind]
        pieces.append((spots[step : step + 1], part, shard[...]))
        if kind < 2:
            wanted.append(shard[nrows : nrows + 1, :nneg].astype(jnp.int32))
    far = nneg * len(wanted)
    names = items[count * side : count * (side + 1)]
    if side:
        names = jnp.concatenate([names, column(jnp.concatenate(wanted, 1))[:far]], 0)
    chosen = chosen_rows(names, pieces)
    out_ref[:count] = partial[count * side : count * (side + 1)] + chosen[:count]
    if side:
        out_ref[count : count + nneg] = panel[...]
        out_ref[count + nneg :] = unit_of(chosen[count:])[0]


def fetch(side, plan, spots, items, partial, panel, shards):
    nneg, width = panel.shape
    count = items.shape[1]
    owners = 1 + len({step for step, _ in plan})
    extra = nneg * owners if side else 0
    return pl.pallas_call(
        functools.partial(fetch_kernel, side, plan),
        out_shape=jax.ShapeDtypeStruct((count + extra, width), F32),
        in_specs=[VMEM] * (4 + len(shards)),
        out_specs=VMEM,
        compiler_params=limit(6),
        cost_estimate=pl.CostEstimate(flops=200_000_000, bytes_accessed=2_000_000, transcendentals=0),
        name="fetch",
    )(spots, items, partial, panel, *shards)


def gather_kernel(first, spots, *refs):
    *grads, out_ref = refs
    count = grads[0].shape[0] - SUBLANES
    tokens = [jnp.concatenate(halves(grad[:count]), 1) for grad in grads]
    tokens = jnp.concatenate(tokens, 0)
    names = jnp.concatenate([grad[count : count + 1] for grad in grads], 1).astype(jnp.int32)
    chips, nrows, part = out_ref.shape
    for step in range(chips):
        base = jnp.concatenate([spots[first + step : first + step + 1, :count] * nrows] * len(grads), 1)
        hot = rows((nrows, names.shape[1])) == names - base
        hot = jnp.where(hot, 1.0, 0.0).astype(BF16)
        both = lax.dot_general(hot, tokens, NN, preferred_element_type=F32)
        out_ref[step] = both[:, :part] + both[:, part:]


def gather(first, spots, grads, nrows, chips):
    return pl.pallas_call(
        functools.partial(gather_kernel, first),
        out_shape=jax.ShapeDtypeStruct((chips, nrows, grads[0].shape[1]), F32),
        in_specs=[VMEM] * (1 + len(grads)),
        out_specs=VMEM,
        compiler_params=limit(4),
        cost_estimate=pl.CostEstimate(flops=150_000_000, bytes_accessed=1_000_000, transcendentals=0),
        name="gather",
    )(spots, *grads)


def swap(value, axis, step, size):
    return lax.ppermute(value, axis, [(i, i ^ step) for i in range(size)])


def direct(item_ids, lengths, buckets, neg_ids, table, w_in, b_in, w_out, rab):
    groups = lax.axis_size("group")
    shards = lax.axis_size("shard")
    group = lax.axis_index("group")
    chips = groups // 2
    nrows = table.shape[0]
    own_side = [group ^ (2 * step) for step in range(chips)]
    scalars = own_side + [index ^ 1 for index in own_side] + [lax.axis_index("shard")]
    where = jnp.stack(scalars).astype(jnp.int32)
    item_row = item_ids.reshape(1, -1)
    neg_row = neg_ids.reshape(1, -1)
    packed = pack(neg_row, table)
    half = nrows // 2
    odd = (lax.axis_index("shard") & 1) == 1
    piece = jnp.where(odd, packed[half:], jnp.concatenate([packed[:half], packed[2 * half :]], 0))
    other_ids = swap(item_row, "group", 1, groups)
    small = small_rows(item_ids, buckets, lengths, neg_ids)
    bias, allowed, valid, items, partial, panel, spots, zeros = prepare(
        small, lengths.size, rab, where, other_ids, packed, neg_ids.size
    )
    plan, panels, after = [], [], zeros
    for step in sorted(range(1, chips), key=lambda step: -step.bit_count()):
        if step.bit_count() > 1:
            near = swap(piece, "group", 2 * step, groups)
            near = near + zeros
            after = near
            plan += [(step, 1), (step, 2)]
            panels += [near, swap(near, "shard", 1, shards)]
        else:
            plan.append((step, 0))
            panels.append(swap(packed, "group", 2 * step, groups))
    *weights, none = weight_halves(w_in, w_out, after)
    spots = spots + none
    other = fetch(1, plan, spots, items, partial, panel, panels)
    mine = fetch(0, plan, spots, items, partial, panel, panels)
    theirs = swap(other, "group", 1, groups)
    loss, *grads = layer(
        theirs,
        other,
        mine,
        weights=weights,
        b_in=b_in,
        bias=bias,
        allowed=allowed,
        valid=valid,
        ids=small[:1],
        spots=spots,
        parts=shards,
    )
    blocks = [grads[0]] + [swap(grads[step], "shard", step, shards) for step in range(1, shards)]
    blocks = [blocks[0], *blocks[:0:-1]]
    other = gather(chips, spots, blocks, nrows, chips)
    own = gather(0, spots, blocks, nrows, chips) + swap(other, "group", 1, groups)
    total = own[0]
    for step in (1,3,2):
        total = total + swap(own[step], "group", 2 * step, groups)
    columns = [total] + [swap(total, "shard", step, shards) for step in range(1, shards)]
    plane_row = spots[-1:]
    wide = []
    for spot in range(shards):
        block = columns[0]
        for step in range(1, shards):
            block = jnp.where((plane_row ^ step) == spot, columns[step], block)
        wide.append(block)
    return jnp.concatenate(wide, 1), loss


def picker_of(wanted, rows_dev):
    flat = wanted.reshape(-1)
    return (flat[:, None] == jnp.arange(rows_dev, dtype=jnp.int32)[None, :]).astype(F32)


def by_request(item_ids, lengths, buckets, neg_ids, table, w_in, b_in, w_out, rab):
    high = lax.Precision.HIGHEST
    small = small_rows(item_ids, buckets, lengths, neg_ids)
    *weights, _ = weight_halves(w_in, w_out, small)
    bias, allowed, valid = prepare(small, lengths.size, rab)
    groups = lax.axis_size("group")
    rows_dev, width = table.shape
    count = item_ids.shape[0]
    capacity = max(2, 2 * count // groups)
    slots = groups * capacity
    owner = item_ids // rows_dev
    member = (owner[:, None] == jnp.arange(groups, dtype=jnp.int32)[None, :]).astype(jnp.int32)
    rank = jnp.sum(member * (jnp.cumsum(member, 0) - 1), 1)
    target_slot = owner * capacity + rank
    requests = (
        jnp.full((slots,), -1, jnp.int32)
        .at[target_slot]
        .set(item_ids % rows_dev)
        .reshape(groups, capacity)
    )
    own_negatives, _ = unit_of(table[neg_ids.reshape(-1) % rows_dev])
    panel_rows = lax.all_gather(own_negatives, "group", axis=0, tiled=True)
    incoming = lax.all_to_all(requests, "group", split_axis=0, concat_axis=0, tiled=True)
    picker = picker_of(incoming, rows_dev)
    served = jnp.dot(picker, table, precision=high).reshape(groups, capacity, width)
    returned = lax.all_to_all(served, "group", split_axis=0, concat_axis=0, tiled=True)
    emb = returned.reshape(slots, width)[target_slot]
    packed = jnp.concatenate([emb, panel_rows], 0)
    loss, d_emb = layer(
        packed,
        weights=weights,
        b_in=b_in,
        bias=bias,
        allowed=allowed,
        valid=valid,
        ids=small[:1],
        spots=jnp.zeros((1, LANES), jnp.int32),
        parts=1,
    )
    outgoing = jnp.zeros((slots, width), F32).at[target_slot].set(d_emb)
    arrived = lax.all_to_all(
        outgoing.reshape(groups, capacity, width), "group", split_axis=0, concat_axis=0, tiled=True
    )
    partial_grad = jnp.dot(picker.T, arrived.reshape(slots, width), precision=high)
    return lax.psum(partial_grad, "shard"), loss


def body(item_ids, seq_lengths, time_buckets, neg_ids, table, w_in, b_in, w_out, rab):
    groups = lax.axis_size("group")
    shards = lax.axis_size("shard")
    width = table.shape[1]
    small = groups in (2, 4, 8, 16) and shards & (shards - 1) == 0 and shards > 1
    small = small and item_ids.shape[0] == LANES and shards * LANES == width
    plan = direct if small else by_request
    grad, loss = plan(
        item_ids, seq_lengths, time_buckets, neg_ids, table, w_in, b_in, w_out, rab
    )
    return grad, loss.reshape(-1)


def solution(mesh):
    in_specs = (
        P(("shard", "group")),
        P(("shard", "group"), None),
        P(("shard", "group")),
        P("shard", "group"),
        P("group", None),
        P(),
        P(),
        P(),
        P(),
    )
    out_specs = (P("group", None), P(("shard", "group")))
    return jax.shard_map(body, mesh=mesh, in_specs=in_specs, out_specs=out_specs, check_vma=False)
```

```python
import functools

import jax
import jax.numpy as jnp
from jax import lax
from jax.experimental import pallas as pl
from jax.experimental.pallas import tpu as pltpu
from jax.sharding import PartitionSpec as P

MOST_LEN = 64
TEMPER = 0.05
LANES = 128
SUBLANES = 8
F32 = jnp.float32
BF16 = jnp.bfloat16
NN = (((1,), (0,)), ((), ()))
NT = (((1,), (1,)), ((), ()))
TN = (((0,), (0,)), ((), ()))
VMEM = pl.BlockSpec(memory_space=pltpu.VMEM)
SMEM = pl.BlockSpec(memory_space=pltpu.SMEM)


def limit(mebibytes):
    return pltpu.CompilerParams(vmem_limit_bytes=mebibytes * 1024 * 1024)


def halves(value):
    high = value.astype(BF16)
    return high, (value - high.astype(F32)).astype(BF16)


def mul(left, right, dims=NN):
    lh, ll = left
    rh, rl = right
    dot = functools.partial(lax.dot_general, dimension_numbers=dims, preferred_element_type=F32)
    both = dot(jnp.concatenate([lh, ll], 0), rh)
    count = lh.shape[0]
    return both[:count] + (both[count:] + dot(lh, rl))


def mul_small(left, right, dims=NN):
    lh, ll = left
    rh, rl = right
    if dims == NN:
        wide = jnp.concatenate([rh, rl], 1)
        right = jnp.concatenate([wide, wide], 0)
    else:
        right = jnp.concatenate([jnp.concatenate([rh, rh], 1), jnp.concatenate([rl, rl], 1)], 0)
    both = lax.dot_general(jnp.concatenate([lh, ll], 1), right, dims, preferred_element_type=F32)
    half = both.shape[1] // 2
    return both[:, :half] + both[:, half:]


def sum_last(value):
    return jnp.sum(value, axis=-1, keepdims=True)


def mean_last(value):
    return jnp.mean(value, axis=-1, keepdims=True)


def lanes(shape):
    return lax.broadcasted_iota(jnp.int32, shape, 1)


def rows(shape):
    return lax.broadcasted_iota(jnp.int32, shape, 0)


def spread(row, count):
    wide = jnp.broadcast_to(row.astype(F32), (count, count))
    return wide.T.astype(jnp.int32)


def column(row):
    short = LANES - row.shape[1]
    if short:
        row = jnp.concatenate([row, jnp.full((1, short), -1, jnp.int32)], 1)
    return spread(row, LANES)


def norm_of(value):
    centered = value - mean_last(value)
    scale = lax.rsqrt(mean_last(centered * centered) + 1e-05)
    return centered * scale, scale


def norm_back(grad, normed, scale):
    return scale * (grad - mean_last(grad) - normed * mean_last(grad * normed))


def unit_of(value):
    scale = lax.rsqrt(sum_last(value * value) + 1e-06)
    return value * scale, scale


def unit_back(grad, united, scale):
    return scale * (grad - united * sum_last(grad * united))


def time_bias(rab, buckets, bias):
    count = buckets.shape[1]
    gap = jnp.abs(buckets - spread(buckets, count))
    heads, nbuck = rab.shape
    for head in range(heads):
        level = jnp.concatenate([rab[head : head + 1, :], jnp.zeros((1, LANES - nbuck), F32)], 1)
        level = jnp.broadcast_to(level, (count, LANES))
        bias[head] = jnp.take_along_axis(level, gap, axis=1)


def masks(lengths, number):
    square = (LANES, LANES)
    place_i, place_j = rows(square), lanes(square)
    upto = jnp.where(place_i <= place_j, spread(lengths, LANES), 0)
    ends = spread(jnp.sum(upto, axis=0, keepdims=True), LANES)
    real = place_i < number
    seg = jnp.sum((real & (place_j >= ends)).astype(jnp.int32), axis=0, keepdims=True)
    following = jnp.sum((real & (place_j + 1 >= ends)).astype(jnp.int32), axis=0, keepdims=True)
    near = (seg == following) & (lanes((1, LANES)) + 1 < LANES)
    allowed = (place_j <= place_i) & (spread(seg, LANES) == seg)
    valid = spread(near.astype(jnp.int32), LANES)
    return jnp.where(allowed, 1.0 / MOST_LEN, 0.0).astype(F32), valid.astype(F32)


def weights_kernel(w_in, w_out, after, in_h, in_l, in_th, in_tl, out_h, out_l, out_th, out_tl, zeros):
    width, hidden = w_in.shape
    zeros[...] = jnp.zeros(zeros.shape, jnp.int32)
    high, low = halves(w_out[...])
    out_h[...], out_l[...] = high, low
    out_th[...], out_tl[...] = high.T, low.T
    for start in range(0, hidden, width):
        span = slice(start, start + width)
        high, low = halves(w_in[:, span])
        in_h[:, span], in_l[:, span] = high, low
        in_th[span, :], in_tl[span, :] = high.T, low.T


def weight_halves(w_in, w_out, after):
    width, hidden = w_in.shape
    shapes = [(width, hidden)] * 2 + [(hidden, width)] * 2 + [(width, width)] * 4
    return pl.pallas_call(
        weights_kernel,
        out_shape=(
            *(jax.ShapeDtypeStruct(shape, BF16) for shape in shapes),
            jax.ShapeDtypeStruct((1, LANES), jnp.int32),
        ),
        in_specs=[VMEM] * 2 + [pl.BlockSpec(memory_space=pl.ANY)],
        out_specs=(VMEM,) * 9,
        compiler_params=limit(8),
        cost_estimate=pl.CostEstimate(flops=4_000_000, bytes_accessed=15_000_000, transcendentals=0),
        name="weight_halves",
    )(w_in, w_out, after)


def prepare_kernel(number, small, rab, bias, allowed, valid):
    allowed[...], valid[...] = masks(small[2:3], number)
    time_bias(rab, small[1:2], bias)


def prepare_own_kernel(number, nneg, where, small, rab, other_ids, shard, *outs):
    *pairs, items, found, panel, spots, zeros = outs
    zeros[...] = jnp.zeros(zeros.shape, F32)
    for index in range(where.shape[0]):
        spots[index : index + 1, :] = jnp.full((1, LANES), where[index], jnp.int32)
    prepare_kernel(number, small, rab, *pairs)
    count = other_ids.shape[1]
    me, other = spread(small[0:1], count), spread(other_ids[...], count)
    items[:count] = me
    items[count:] = other
    names = jnp.concatenate([me, other, spread(small[3:4], LANES)[:nneg]], 0)
    chosen = chosen_rows(names, [(where[0], None, shard[...])])
    found[...] = chosen[: 2 * count]
    panel[...] = unit_of(chosen[2 * count :])[0]


def small_rows(*values):
    total = 0
    for row, value in enumerate(values):
        spots = [(row, len(values) - 1 - row, 0), (0, LANES - value.size, 0)]
        total = total + lax.pad(value.reshape(1, -1), jnp.int32(0), spots)
    return total


def prepare(small, number, rab, where=None, other_ids=None, shard=None, nneg=0):
    count = small.shape[1]
    heads = rab.shape[0]
    sds = jax.ShapeDtypeStruct
    outs = (sds((heads, count, count), F32), *(sds((count, count), F32),) * 2)
    kernel, args, specs = functools.partial(prepare_kernel, number), (small, rab), []
    if where is not None:
        kernel, specs = functools.partial(prepare_own_kernel, number, nneg), [SMEM]
        args = (where, *args, other_ids, shard)
        width = shard.shape[1]
        outs += (
            sds((2 * count, count), jnp.int32),
            sds((2 * count, width), F32),
            sds((nneg, width), F32),
            sds((where.shape[0], LANES), jnp.int32),
            sds((1, width), F32),
        )
    return pl.pallas_call(
        kernel,
        out_shape=outs,
        in_specs=specs + [VMEM] * (len(args) - len(specs)),
        out_specs=(VMEM,) * len(outs),
        compiler_params=limit(6),
        cost_estimate=pl.CostEstimate(flops=200_000_000, bytes_accessed=2_000_000, transcendentals=0),
        name="prepare",
    )(*args)


def layer_kernel(pieces, spots, *refs):
    packed = refs[:pieces]
    in_h, in_l, in_th, in_tl, out_h, out_l, out_th, out_tl = refs[pieces : pieces + 8]
    b_in, bias, allowed_ref, valid_ref, ids = refs[pieces + 8 : pieces + 13]
    loss_ref = refs[pieces + 13]
    grads = refs[pieces + 14 :]
    heads, count, _ = bias.shape
    width = in_h.shape[0]
    each = width // heads
    emb = packed[0][:count]
    if pieces > 1:
        emb = emb + packed[2][...]
    allowed = allowed_ref[...]
    valid = valid_ref[:, :1]
    square = (count, count)
    place_i, place_j = rows(square), lanes(square)
    xn, x_scale = norm_of(emb)
    w_out = (out_h[...], out_l[...])
    xn_parts = halves(xn)
    hidden, slope = {}, {}
    for part in (2, 3, 1, 0):
        span = slice(width * part, width * (part + 1))
        pre = mul(xn_parts, (in_h[:, span], in_l[:, span])) + b_in[:, span]
        sig = jax.nn.sigmoid(pre)
        hidden[part] = pre * sig
        slope[part] = sig * (1.0 + pre * (1.0 - sig))
    upart = hidden[0]
    kept = []
    mixed = []
    for head in range(heads):
        vh, qh, kh = (
            halves(hidden[part][:, each * head : each * (head + 1)])
            for part in (1, 2, 3)
        )
        score = mul_small(qh, kh, NT) * each ** (-0.5) + bias[head]
        gate = jax.nn.sigmoid(score)
        weight = score * gate * allowed
        bend = gate * (1.0 + score * (1.0 - gate)) * allowed
        mixed.append(mul_small(halves(weight), vh))
        kept.append((vh, qh, kh, halves(weight.T), bend))
    yn, y_scale = norm_of(jnp.concatenate(mixed, axis=1))
    out = mul(halves(yn * upart), w_out) + emb
    states, s_scale = unit_of(out)
    united, e_scale = unit_of(emb)
    last = rows((count, width)) == count - 1
    target = jnp.where(last, 0.0, pltpu.roll(united, count - 1, 0))
    positive = sum_last(states * target) * (1.0 / TEMPER)
    expos = jnp.exp(positive)
    state_parts = halves(states)
    panel = halves(jnp.concatenate([piece[count:] for piece in packed[:2]], 0))
    exps = jnp.exp(mul(state_parts, panel, NT) * (1.0 / TEMPER))
    zneg = sum_last(exps)
    pulled = mul(halves(exps), panel)
    total = expos + zneg
    loss = valid * (jnp.log(total) - positive)
    loss_ref[...] = jnp.sum(jnp.where(place_i == place_j, loss, 0.0), axis=0, keepdims=True)
    share = valid * (expos / total - 1.0) * (1.0 / TEMPER)
    d_states = share * target + pulled * (valid / total * (1.0 / TEMPER))
    d_out = unit_back(d_states, states, s_scale)
    first = rows((count, width)) == 0
    d_next = jnp.where(first, 0.0, pltpu.roll(share * states, 1, 0))
    d_emb = d_out + unit_back(d_next, united, e_scale)
    d_gated = mul(halves(d_out), (out_th[...], out_tl[...]))
    d_mixed = norm_back(d_gated * upart, yn, y_scale)

    def input_grad(part, grad):
        span = slice(width * part, width * (part + 1))
        return mul(halves(grad * slope[part]), (in_th[span], in_tl[span]))

    d_xn = input_grad(0, d_gated * yn)
    d_v, d_q, d_k = [], [], []
    for head in range(heads):
        vh, qh, kh, weight_t, bend = kept[head]
        d_mh = halves(d_mixed[:, each * head : each * (head + 1)])
        d_v.append(mul_small(weight_t, d_mh))
        d_score = mul_small(d_mh, vh, NT) * bend * each ** (-0.5)
        d_q.append(mul_small(halves(d_score), kh))
        d_k.append(mul_small(halves(d_score.T), qh))
    for part, grad in ((1, d_v), (2, d_q), (3, d_k)):
        d_xn = d_xn + input_grad(part, jnp.concatenate(grad, axis=1))
    d_emb = d_emb + norm_back(d_xn, xn, x_scale)
    if len(grads) == 1:
        grads[0][...] = d_emb
        return
    part = width // len(grads)
    plane = spots[spots.shape[0] - 1 :, :part]
    for step, out_ref in enumerate(grads):
        block = d_emb[:, :part]
        for spot in range(1, len(grads)):
            mine = (plane ^ step) == spot
            block = jnp.where(mine, d_emb[:, part * spot : part * (spot + 1)], block)
        out_ref[:count] = block
        out_ref[count:] = jnp.broadcast_to(ids[...].astype(F32), (SUBLANES, part))


def layer(*packed, weights, b_in, bias, allowed, valid, ids, spots, parts):
    heads, count, _ = bias.shape
    extra = SUBLANES if parts > 1 else 0
    width = weights[0].shape[0]
    sds = jax.ShapeDtypeStruct
    return pl.pallas_call(
        functools.partial(layer_kernel, len(packed)),
        out_shape=(sds((1, count), F32),) + (sds((count + extra, width // parts), F32),) * parts,
        in_specs=[VMEM] * (len(packed) + 14),
        out_specs=(VMEM,) * (1 + parts),
        compiler_params=limit(14 if parts > 1 else 40),
        cost_estimate=pl.CostEstimate(
            flops=2_500_000_000, bytes_accessed=8_000_000, transcendentals=400_000
        ),
        name="layer",
    )(spots, *packed, *weights, b_in.reshape(1, -1), bias, allowed, valid, ids)


def pack(neg_ids, table):
    nrows, width = table.shape
    body = lax.pad(table, jnp.float32(0), [(0, SUBLANES, 0), (0, 0, 0)])
    tile = [(nrows, SUBLANES - 1, 0), (0, width - neg_ids.shape[1], 0)]
    return body + lax.pad(neg_ids, jnp.int32(0), tile).astype(F32)


def chosen_rows(names, pieces):
    place = jnp.full(names.shape, -1, jnp.int32)
    offset = 0
    for owner, part, held in pieces:
        nrows = held.shape[0] - SUBLANES
        if part is None:
            spot = names - owner * nrows
        else:
            spot = names - (owner * 2 + part) * nrows
        place = jnp.where((spot >= 0) & (spot < nrows), spot + offset, place)
        offset += held.shape[0]
    rest = -offset % LANES
    held = [piece[2] for piece in pieces]
    if rest:
        held.append(jnp.zeros((rest, held[0].shape[1]), F32))
    column = lanes(names.shape)
    hot = [place == column + start for start in range(0, offset + rest, LANES)]
    hot = jnp.where(jnp.concatenate(hot, 1), 1.0, 0.0).astype(BF16)
    high, low = halves(jnp.concatenate(held, 0))
    dot = functools.partial(lax.dot_general, dimension_numbers=NN, preferred_element_type=F32)
    return dot(hot, high) + dot(hot, low)


def fetch_kernel(side, plan, spots, items, partial, panel, *refs):
    *shards, out_ref = refs
    nneg = panel.shape[0]
    count = items.shape[1]
    odd = spots[spots.shape[0] - 1 :, :] & 1
    pieces, wanted = [], []
    for (step, kind), shard in zip(plan, shards):
        nrows = shard.shape[0] - SUBLANES
        part = {0: None, 1: odd, 2: 1 - odd}[kind]
        pieces.append((spots[step : step + 1], part, shard[...]))
        if kind < 2:
            wanted.append(shard[nrows : nrows + 1, :nneg].astype(jnp.int32))
    far = nneg * len(wanted)
    names = items[count * side : count * (side + 1)]
    if side:
        names = jnp.concatenate([names, column(jnp.concatenate(wanted, 1))[:far]], 0)
    chosen = chosen_rows(names, pieces)
    out_ref[:count] = partial[count * side : count * (side + 1)] + chosen[:count]
    if side:
        out_ref[count : count + nneg] = panel[...]
        out_ref[count + nneg :] = unit_of(chosen[count:])[0]


def fetch(side, plan, spots, items, partial, panel, shards):
    nneg, width = panel.shape
    count = items.shape[1]
    owners = 1 + len({step for step, _ in plan})
    extra = nneg * owners if side else 0
    return pl.pallas_call(
        functools.partial(fetch_kernel, side, plan),
        out_shape=jax.ShapeDtypeStruct((count + extra, width), F32),
        in_specs=[VMEM] * (4 + len(shards)),
        out_specs=VMEM,
        compiler_params=limit(6),
        cost_estimate=pl.CostEstimate(flops=200_000_000, bytes_accessed=2_000_000, transcendentals=0),
        name="fetch",
    )(spots, items, partial, panel, *shards)


def gather_kernel(first, spots, *refs):
    *grads, out_ref = refs
    count = grads[0].shape[0] - SUBLANES
    tokens = [jnp.concatenate(halves(grad[:count]), 1) for grad in grads]
    tokens = jnp.concatenate(tokens, 0)
    names = jnp.concatenate([grad[count : count + 1] for grad in grads], 1).astype(jnp.int32)
    chips, nrows, part = out_ref.shape
    for step in range(chips):
        base = jnp.concatenate([spots[first + step : first + step + 1, :count] * nrows] * len(grads), 1)
        hot = rows((nrows, names.shape[1])) == names - base
        hot = jnp.where(hot, 1.0, 0.0).astype(BF16)
        both = lax.dot_general(hot, tokens, NN, preferred_element_type=F32)
        out_ref[step] = both[:, :part] + both[:, part:]


def gather(first, spots, grads, nrows, chips):
    return pl.pallas_call(
        functools.partial(gather_kernel, first),
        out_shape=jax.ShapeDtypeStruct((chips, nrows, grads[0].shape[1]), F32),
        in_specs=[VMEM] * (1 + len(grads)),
        out_specs=VMEM,
        compiler_params=limit(4),
        cost_estimate=pl.CostEstimate(flops=150_000_000, bytes_accessed=1_000_000, transcendentals=0),
        name="gather",
    )(spots, *grads)


def swap(value, axis, step, size):
    return lax.ppermute(value, axis, [(i, i ^ step) for i in range(size)])


def direct(item_ids, lengths, buckets, neg_ids, table, w_in, b_in, w_out, rab):
    groups = lax.axis_size("group")
    shards = lax.axis_size("shard")
    group = lax.axis_index("group")
    chips = groups // 2
    nrows = table.shape[0]
    own_side = [group ^ (2 * step) for step in range(chips)]
    scalars = own_side + [index ^ 1 for index in own_side] + [lax.axis_index("shard")]
    where = jnp.stack(scalars).astype(jnp.int32)
    item_row = item_ids.reshape(1, -1)
    neg_row = neg_ids.reshape(1, -1)
    packed = pack(neg_row, table)
    half = nrows // 2
    odd = (lax.axis_index("shard") & 1) == 1
    piece = jnp.where(odd, packed[half:], jnp.concatenate([packed[:half], packed[2 * half :]], 0))
    other_ids = swap(item_row, "group", 1, groups)
    small = small_rows(item_ids, buckets, lengths, neg_ids)
    bias, allowed, valid, items, partial, panel, spots, zeros = prepare(
        small, lengths.size, rab, where, other_ids, packed, neg_ids.size
    )
    plan, panels, after = [], [], zeros
    for step in sorted(range(1, chips), key=lambda step: -step.bit_count()):
        if step.bit_count() > 1:
            near = swap(piece, "group", 2 * step, groups)
            near = near + zeros
            after = near
            plan += [(step, 1), (step, 2)]
            panels += [near, swap(near, "shard", 1, shards)]
        else:
            plan.append((step, 0))
            panels.append(swap(packed, "group", 2 * step, groups))
    *weights, none = weight_halves(w_in, w_out, after)
    spots = spots + none
    other = fetch(1, plan, spots, items, partial, panel, panels)
    mine = fetch(0, plan, spots, items, partial, panel, panels)
    theirs = swap(other, "group", 1, groups)
    loss, *grads = layer(
        theirs,
        other,
        mine,
        weights=weights,
        b_in=b_in,
        bias=bias,
        allowed=allowed,
        valid=valid,
        ids=small[:1],
        spots=spots,
        parts=shards,
    )
    blocks = [grads[0]] + [swap(grads[step], "shard", step, shards) for step in range(1, shards)]
    blocks = [blocks[0], blocks[-1], *blocks[1:-1]]
    other = gather(chips, spots, blocks, nrows, chips)
    own = gather(0, spots, blocks, nrows, chips) + swap(other, "group", 1, groups)
    total = own[0]
    for step in range(chips - 1, 0, -1):
        total = total + swap(own[step], "group", 2 * step, groups)
    columns = [total] + [swap(total, "shard", step, shards) for step in range(1, shards)]
    plane_row = spots[-1:]
    wide = []
    for spot in range(shards):
        block = columns[0]
        for step in (*range(1, shards, 2), *range(2, shards, 2)):
            block = jnp.where((plane_row ^ step) == spot, columns[step], block)
        wide.append(block)
    return jnp.concatenate(wide, 1), loss


def picker_of(wanted, rows_dev):
    flat = wanted.reshape(-1)
    return (flat[:, None] == jnp.arange(rows_dev, dtype=jnp.int32)[None, :]).astype(F32)


def by_request(item_ids, lengths, buckets, neg_ids, table, w_in, b_in, w_out, rab):
    high = lax.Precision.HIGHEST
    small = small_rows(item_ids, buckets, lengths, neg_ids)
    *weights, _ = weight_halves(w_in, w_out, small)
    bias, allowed, valid = prepare(small, lengths.size, rab)
    groups = lax.axis_size("group")
    rows_dev, width = table.shape
    count = item_ids.shape[0]
    capacity = max(2, 2 * count // groups)
    slots = groups * capacity
    owner = item_ids // rows_dev
    member = (owner[:, None] == jnp.arange(groups, dtype=jnp.int32)[None, :]).astype(jnp.int32)
    rank = jnp.sum(member * (jnp.cumsum(member, 0) - 1), 1)
    target_slot = owner * capacity + rank
    requests = (
        jnp.full((slots,), -1, jnp.int32)
        .at[target_slot]
        .set(item_ids % rows_dev)
        .reshape(groups, capacity)
    )
    own_negatives, _ = unit_of(table[neg_ids.reshape(-1) % rows_dev])
    panel_rows = lax.all_gather(own_negatives, "group", axis=0, tiled=True)
    incoming = lax.all_to_all(requests, "group", split_axis=0, concat_axis=0, tiled=True)
    picker = picker_of(incoming, rows_dev)
    served = jnp.dot(picker, table, precision=high).reshape(groups, capacity, width)
    returned = lax.all_to_all(served, "group", split_axis=0, concat_axis=0, tiled=True)
    emb = returned.reshape(slots, width)[target_slot]
    packed = jnp.concatenate([emb, panel_rows], 0)
    loss, d_emb = layer(
        packed,
        weights=weights,
        b_in=b_in,
        bias=bias,
        allowed=allowed,
        valid=valid,
        ids=small[:1],
        spots=jnp.zeros((1, LANES), jnp.int32),
        parts=1,
    )
    outgoing = jnp.zeros((slots, width), F32).at[target_slot].set(d_emb)
    arrived = lax.all_to_all(
        outgoing.reshape(groups, capacity, width), "group", split_axis=0, concat_axis=0, tiled=True
    )
    partial_grad = jnp.dot(picker.T, arrived.reshape(slots, width), precision=high)
    return lax.psum(partial_grad, "shard"), loss


def body(item_ids, seq_lengths, time_buckets, neg_ids, table, w_in, b_in, w_out, rab):
    groups = lax.axis_size("group")
    shards = lax.axis_size("shard")
    width = table.shape[1]
    small = groups in (2, 4, 8, 16) and shards & (shards - 1) == 0 and shards > 1
    small = small and item_ids.shape[0] == LANES and shards * LANES == width
    plan = direct if small else by_request
    grad, loss = plan(
        item_ids, seq_lengths, time_buckets, neg_ids, table, w_in, b_in, w_out, rab
    )
    return grad, loss.reshape(-1)


def solution(mesh):
    in_specs = (
        P(("shard", "group")),
        P(("shard", "group"), None),
        P(("shard", "group")),
        P("shard", "group"),
        P("group", None),
        P(),
        P(),
        P(),
        P(),
    )
    out_specs = (P("group", None), P(("shard", "group")))
    return jax.shard_map(body, mesh=mesh, in_specs=in_specs, out_specs=out_specs, check_vma=False)
```

```python
import functools

import jax
import jax.numpy as jnp
from jax import lax
from jax.experimental import pallas as pl
from jax.experimental.pallas import tpu as pltpu
from jax.sharding import PartitionSpec as P

MOST_LEN = 64
TEMPER = 0.05
LANES = 128
SUBLANES = 8
F32 = jnp.float32
BF16 = jnp.bfloat16
NN = (((1,), (0,)), ((), ()))
NT = (((1,), (1,)), ((), ()))
TN = (((0,), (0,)), ((), ()))
VMEM = pl.BlockSpec(memory_space=pltpu.VMEM)
SMEM = pl.BlockSpec(memory_space=pltpu.SMEM)


def limit(mebibytes):
    return pltpu.CompilerParams(vmem_limit_bytes=mebibytes * 1024 * 1024)


def halves(value):
    high = value.astype(BF16)
    return high, (value - high.astype(F32)).astype(BF16)


def mul(left, right, dims=NN):
    lh, ll = left
    rh, rl = right
    dot = functools.partial(lax.dot_general, dimension_numbers=dims, preferred_element_type=F32)
    both = dot(jnp.concatenate([lh, ll], 0), rh)
    count = lh.shape[0]
    return both[:count] + (both[count:] + dot(lh, rl))


def mul_small(left, right, dims=NN):
    lh, ll = left
    rh, rl = right
    if dims == NN:
        wide = jnp.concatenate([rh, rl], 1)
        right = jnp.concatenate([wide, wide], 0)
    else:
        right = jnp.concatenate([jnp.concatenate([rh, rh], 1), jnp.concatenate([rl, rl], 1)], 0)
    both = lax.dot_general(jnp.concatenate([lh, ll], 1), right, dims, preferred_element_type=F32)
    half = both.shape[1] // 2
    return both[:, :half] + both[:, half:]


def sum_last(value):
    return jnp.sum(value, axis=-1, keepdims=True)


def mean_last(value):
    return jnp.mean(value, axis=-1, keepdims=True)


def lanes(shape):
    return lax.broadcasted_iota(jnp.int32, shape, 1)


def rows(shape):
    return lax.broadcasted_iota(jnp.int32, shape, 0)


def spread(row, count):
    wide = jnp.broadcast_to(row.astype(F32), (count, count))
    return wide.T.astype(jnp.int32)


def column(row):
    short = LANES - row.shape[1]
    if short:
        row = jnp.concatenate([row, jnp.full((1, short), -1, jnp.int32)], 1)
    return spread(row, LANES)


def norm_of(value):
    centered = value - mean_last(value)
    scale = lax.rsqrt(mean_last(centered * centered) + 1e-05)
    return centered * scale, scale


def norm_back(grad, normed, scale):
    return scale * (grad - mean_last(grad) - normed * mean_last(grad * normed))


def unit_of(value):
    scale = lax.rsqrt(sum_last(value * value) + 1e-06)
    return value * scale, scale


def unit_back(grad, united, scale):
    return scale * (grad - united * sum_last(grad * united))


def time_bias(rab, buckets, bias):
    count = buckets.shape[1]
    gap = jnp.abs(buckets - spread(buckets, count))
    heads, nbuck = rab.shape
    for head in range(heads):
        level = jnp.concatenate([rab[head : head + 1, :], jnp.zeros((1, LANES - nbuck), F32)], 1)
        level = jnp.broadcast_to(level, (count, LANES))
        bias[head] = jnp.take_along_axis(level, gap, axis=1)


def masks(lengths, number):
    square = (LANES, LANES)
    place_i, place_j = rows(square), lanes(square)
    upto = jnp.where(place_i <= place_j, spread(lengths, LANES), 0)
    ends = spread(jnp.sum(upto, axis=0, keepdims=True), LANES)
    real = place_i < number
    seg = jnp.sum((real & (place_j >= ends)).astype(jnp.int32), axis=0, keepdims=True)
    following = jnp.sum((real & (place_j + 1 >= ends)).astype(jnp.int32), axis=0, keepdims=True)
    near = (seg == following) & (lanes((1, LANES)) + 1 < LANES)
    allowed = (place_j <= place_i) & (spread(seg, LANES) == seg)
    valid = spread(near.astype(jnp.int32), LANES)
    return jnp.where(allowed, 1.0 / MOST_LEN, 0.0).astype(F32), valid.astype(F32)


def weights_kernel(w_in, w_out, after, in_h, in_l, in_th, in_tl, out_h, out_l, out_th, out_tl, zeros):
    width, hidden = w_in.shape
    zeros[...] = jnp.zeros(zeros.shape, jnp.int32)
    high, low = halves(w_out[...])
    out_h[...], out_l[...] = high, low
    out_th[...], out_tl[...] = high.T, low.T
    for start in range(0, hidden, width):
        span = slice(start, start + width)
        high, low = halves(w_in[:, span])
        in_h[:, span], in_l[:, span] = high, low
        in_th[span, :], in_tl[span, :] = high.T, low.T


def weight_halves(w_in, w_out, after):
    width, hidden = w_in.shape
    shapes = [(width, hidden)] * 2 + [(hidden, width)] * 2 + [(width, width)] * 4
    return pl.pallas_call(
        weights_kernel,
        out_shape=(
            *(jax.ShapeDtypeStruct(shape, BF16) for shape in shapes),
            jax.ShapeDtypeStruct((1, LANES), jnp.int32),
        ),
        in_specs=[VMEM] * 2 + [pl.BlockSpec(memory_space=pl.ANY)],
        out_specs=(VMEM,) * 9,
        compiler_params=limit(8),
        cost_estimate=pl.CostEstimate(flops=4_000_000, bytes_accessed=15_000_000, transcendentals=0),
        name="weight_halves",
    )(w_in, w_out, after)


def prepare_kernel(number, small, rab, bias, allowed, valid):
    allowed[...], valid[...] = masks(small[2:3], number)
    time_bias(rab, small[1:2], bias)


def prepare_own_kernel(number, nneg, where, small, rab, other_ids, shard, *outs):
    *pairs, items, found, panel, spots, zeros = outs
    zeros[...] = jnp.zeros(zeros.shape, F32)
    for index in range(where.shape[0]):
        spots[index : index + 1, :] = jnp.full((1, LANES), where[index], jnp.int32)
    prepare_kernel(number, small, rab, *pairs)
    count = other_ids.shape[1]
    me, other = spread(small[0:1], count), spread(other_ids[...], count)
    items[:count] = me
    items[count:] = other
    names = jnp.concatenate([me, other, spread(small[3:4], LANES)[:nneg]], 0)
    chosen = chosen_rows(names, [(where[0], None, shard[...])])
    found[...] = chosen[: 2 * count]
    panel[...] = unit_of(chosen[2 * count :])[0]


def small_rows(*values):
    total = 0
    for row, value in enumerate(values):
        spots = [(row, len(values) - 1 - row, 0), (0, LANES - value.size, 0)]
        total = total + lax.pad(value.reshape(1, -1), jnp.int32(0), spots)
    return total


def prepare(small, number, rab, where=None, other_ids=None, shard=None, nneg=0):
    count = small.shape[1]
    heads = rab.shape[0]
    sds = jax.ShapeDtypeStruct
    outs = (sds((heads, count, count), F32), *(sds((count, count), F32),) * 2)
    kernel, args, specs = functools.partial(prepare_kernel, number), (small, rab), []
    if where is not None:
        kernel, specs = functools.partial(prepare_own_kernel, number, nneg), [SMEM]
        args = (where, *args, other_ids, shard)
        width = shard.shape[1]
        outs += (
            sds((2 * count, count), jnp.int32),
            sds((2 * count, width), F32),
            sds((nneg, width), F32),
            sds((where.shape[0], LANES), jnp.int32),
            sds((1, width), F32),
        )
    return pl.pallas_call(
        kernel,
        out_shape=outs,
        in_specs=specs + [VMEM] * (len(args) - len(specs)),
        out_specs=(VMEM,) * len(outs),
        compiler_params=limit(6),
        cost_estimate=pl.CostEstimate(flops=200_000_000, bytes_accessed=2_000_000, transcendentals=0),
        name="prepare",
    )(*args)


def layer_kernel(pieces, spots, *refs):
    packed = refs[:pieces]
    in_h, in_l, in_th, in_tl, out_h, out_l, out_th, out_tl = refs[pieces : pieces + 8]
    b_in, bias, allowed_ref, valid_ref, ids = refs[pieces + 8 : pieces + 13]
    loss_ref = refs[pieces + 13]
    grads = refs[pieces + 14 :]
    heads, count, _ = bias.shape
    width = in_h.shape[0]
    each = width // heads
    emb = packed[0][:count]
    if pieces > 1:
        emb = emb + packed[2][...]
    allowed = allowed_ref[...]
    valid = valid_ref[:, :1]
    square = (count, count)
    place_i, place_j = rows(square), lanes(square)
    xn, x_scale = norm_of(emb)
    w_out = (out_h[...], out_l[...])
    xn_parts = halves(xn)
    hidden, slope = {}, {}

    def project(start, size):
        span = slice(start, start + size)
        pre = mul(xn_parts, (in_h[:, span], in_l[:, span])) + b_in[:, span]
        sig = jax.nn.sigmoid(pre)
        return pre * sig, sig * (1.0 + pre * (1.0 - sig))

    for part in (2, 3, 1):
        hidden[part], slope[part] = project(width * part, width)
    gates = []
    kept = []
    mixed = []
    for head in range(heads):
        if head % 2 == 0:
            gates.append(project(each * head, 2 * each))
        vh, qh, kh = (
            halves(hidden[part][:, each * head : each * (head + 1)])
            for part in (1, 2, 3)
        )
        score = mul_small(qh, kh, NT) * each ** (-0.5) + bias[head]
        gate = jax.nn.sigmoid(score)
        weight = score * gate * allowed
        bend = gate * (1.0 + score * (1.0 - gate)) * allowed
        mixed.append(mul_small(halves(weight), vh))
        kept.append((vh, qh, kh, halves(weight.T), bend))
    upart, slope[0] = (jnp.concatenate(pair, axis=1) for pair in zip(*gates))
    yn, y_scale = norm_of(jnp.concatenate(mixed, axis=1))
    out = mul(halves(yn * upart), w_out) + emb
    states, s_scale = unit_of(out)
    united, e_scale = unit_of(emb)
    last = rows((count, width)) == count - 1
    target = jnp.where(last, 0.0, pltpu.roll(united, count - 1, 0))
    positive = sum_last(states * target) * (1.0 / TEMPER)
    expos = jnp.exp(positive)
    state_parts = halves(states)
    panel = halves(jnp.concatenate([piece[count:] for piece in packed[:2]], 0))
    logits = mul(state_parts, panel, NT) * (1.0 / TEMPER)
    exps = jnp.exp(logits)
    zneg = sum_last(exps)
    tilt = sum_last(exps * logits)
    pulled = mul(halves(exps), panel)
    total = expos + zneg
    loss = valid * (jnp.log(total) - positive)
    loss_ref[...] = jnp.sum(jnp.where(place_i == place_j, loss, 0.0), axis=0, keepdims=True)
    share = valid * (expos / total - 1.0) * (1.0 / TEMPER)
    d_states = share * target + pulled * (valid / total * (1.0 / TEMPER))
    d_out = s_scale * (d_states - states * (share * TEMPER * positive + tilt * (valid / total)))
    first = rows((count, width)) == 0
    d_next = jnp.where(first, 0.0, pltpu.roll(share * states, 1, 0))
    d_emb = d_out + unit_back(d_next, united, e_scale)
    d_gated = mul(halves(d_out), (out_th[...], out_tl[...]))
    d_mixed = norm_back(d_gated * upart, yn, y_scale)

    def input_grad(part, start, grad):
        span = slice(width * part + start, width * part + start + 2 * each)
        return mul(halves(grad * slope[part][:, start : start + 2 * each]), (in_th[span], in_tl[span]))

    d_gate = d_gated * yn
    d_xn = jnp.zeros((count, width), F32)
    for start in range(0, width, 2 * each):
        d_xn = d_xn + input_grad(0, start, d_gate[:, start : start + 2 * each])
        d_v, d_q, d_k = [], [], []
        for head in (start // each, start // each + 1):
            vh, qh, kh, weight_t, bend = kept[head]
            d_mh = halves(d_mixed[:, each * head : each * (head + 1)])
            d_v.append(mul_small(weight_t, d_mh))
            d_score = mul_small(d_mh, vh, NT) * bend * each ** (-0.5)
            d_q.append(mul_small(halves(d_score), kh))
            d_k.append(mul_small(halves(d_score.T), qh))
        for part, grad in ((1, d_v), (2, d_q), (3, d_k)):
            d_xn = d_xn + input_grad(part, start, jnp.concatenate(grad, axis=1))
    d_emb = d_emb + norm_back(d_xn, xn, x_scale)
    if len(grads) == 1:
        grads[0][...] = d_emb
        return
    part = width // len(grads)
    plane = spots[spots.shape[0] - 1 :, :part]
    for step, out_ref in enumerate(grads):
        block = d_emb[:, :part]
        for spot in range(1, len(grads)):
            mine = (plane ^ step) == spot
            block = jnp.where(mine, d_emb[:, part * spot : part * (spot + 1)], block)
        out_ref[:count] = block
        out_ref[count:] = jnp.broadcast_to(ids[...].astype(F32), (SUBLANES, part))


def layer(*packed, weights, b_in, bias, allowed, valid, ids, spots, parts):
    heads, count, _ = bias.shape
    extra = SUBLANES if parts > 1 else 0
    width = weights[0].shape[0]
    sds = jax.ShapeDtypeStruct
    return pl.pallas_call(
        functools.partial(layer_kernel, len(packed)),
        out_shape=(sds((1, count), F32),) + (sds((count + extra, width // parts), F32),) * parts,
        in_specs=[VMEM] * (len(packed) + 14),
        out_specs=(VMEM,) * (1 + parts),
        compiler_params=limit(14 if parts > 1 else 40),
        cost_estimate=pl.CostEstimate(
            flops=2_500_000_000, bytes_accessed=8_000_000, transcendentals=400_000
        ),
        name="layer",
    )(spots, *packed, *weights, b_in.reshape(1, -1), bias, allowed, valid, ids)


def pack(neg_ids, table):
    nrows, width = table.shape
    body = lax.pad(table, jnp.float32(0), [(0, SUBLANES, 0), (0, 0, 0)])
    tile = [(nrows, SUBLANES - 1, 0), (0, width - neg_ids.shape[1], 0)]
    return body + lax.pad(neg_ids, jnp.int32(0), tile).astype(F32)


def chosen_rows(names, pieces):
    place = jnp.full(names.shape, -1, jnp.int32)
    offset = 0
    for owner, part, held in pieces:
        nrows = held.shape[0] - SUBLANES
        if part is None:
            spot = names - owner * nrows
        else:
            spot = names - (owner * 2 + part) * nrows
        place = jnp.where((spot >= 0) & (spot < nrows), spot + offset, place)
        offset += held.shape[0]
    rest = -offset % LANES
    held = [piece[2] for piece in pieces]
    if rest:
        held.append(jnp.zeros((rest, held[0].shape[1]), F32))
    column = lanes(names.shape)
    hot = [place == column + start for start in range(0, offset + rest, LANES)]
    hot = jnp.where(jnp.concatenate(hot, 1), 1.0, 0.0).astype(BF16)
    high, low = halves(jnp.concatenate(held, 0))
    dot = functools.partial(lax.dot_general, dimension_numbers=NN, preferred_element_type=F32)
    return dot(hot, high) + dot(hot, low)


def fetch_kernel(side, plan, spots, items, partial, panel, *refs):
    *shards, out_ref = refs
    nneg = panel.shape[0]
    count = items.shape[1]
    odd = spots[spots.shape[0] - 1 :, :] & 1
    pieces, wanted = [], []
    for (step, kind), shard in zip(plan, shards):
        nrows = shard.shape[0] - SUBLANES
        part = {0: None, 1: odd, 2: 1 - odd}[kind]
        pieces.append((spots[step : step + 1], part, shard[...]))
        if kind < 2:
            wanted.append(shard[nrows : nrows + 1, :nneg].astype(jnp.int32))
    far = nneg * len(wanted)
    names = items[count * side : count * (side + 1)]
    if side:
        names = jnp.concatenate([names, column(jnp.concatenate(wanted, 1))[:far]], 0)
    chosen = chosen_rows(names, pieces)
    out_ref[:count] = partial[count * side : count * (side + 1)] + chosen[:count]
    if side:
        out_ref[count : count + nneg] = panel[...]
        out_ref[count + nneg :] = unit_of(chosen[count:])[0]


def fetch(side, plan, spots, items, partial, panel, shards):
    nneg, width = panel.shape
    count = items.shape[1]
    owners = 1 + len({step for step, _ in plan})
    extra = nneg * owners if side else 0
    return pl.pallas_call(
        functools.partial(fetch_kernel, side, plan),
        out_shape=jax.ShapeDtypeStruct((count + extra, width), F32),
        in_specs=[VMEM] * (4 + len(shards)),
        out_specs=VMEM,
        compiler_params=limit(6),
        cost_estimate=pl.CostEstimate(flops=200_000_000, bytes_accessed=2_000_000, transcendentals=0),
        name="fetch",
    )(spots, items, partial, panel, *shards)


def gather_kernel(first, spots, *refs):
    *grads, out_ref = refs
    count = grads[0].shape[0] - SUBLANES
    tokens = [jnp.concatenate(halves(grad[:count]), 1) for grad in grads]
    tokens = jnp.concatenate(tokens, 0)
    names = jnp.concatenate([grad[count : count + 1] for grad in grads], 1).astype(jnp.int32)
    chips, nrows, part = out_ref.shape
    for step in range(chips):
        base = jnp.concatenate([spots[first + step : first + step + 1, :count] * nrows] * len(grads), 1)
        hot = rows((nrows, names.shape[1])) == names - base
        hot = jnp.where(hot, 1.0, 0.0).astype(BF16)
        both = lax.dot_general(hot, tokens, NN, preferred_element_type=F32)
        out_ref[step] = both[:, :part] + both[:, part:]


def gather(first, spots, grads, nrows, chips):
    return pl.pallas_call(
        functools.partial(gather_kernel, first),
        out_shape=jax.ShapeDtypeStruct((chips, nrows, grads[0].shape[1]), F32),
        in_specs=[VMEM] * (1 + len(grads)),
        out_specs=VMEM,
        compiler_params=limit(4),
        cost_estimate=pl.CostEstimate(flops=150_000_000, bytes_accessed=1_000_000, transcendentals=0),
        name="gather",
    )(spots, *grads)


def swap(value, axis, step, size):
    return lax.ppermute(value, axis, [(i, i ^ step) for i in range(size)])


def direct(item_ids, lengths, buckets, neg_ids, table, w_in, b_in, w_out, rab):
    groups = lax.axis_size("group")
    shards = lax.axis_size("shard")
    group = lax.axis_index("group")
    chips = groups // 2
    nrows = table.shape[0]
    own_side = [group ^ (2 * step) for step in range(chips)]
    scalars = own_side + [index ^ 1 for index in own_side] + [lax.axis_index("shard")]
    where = jnp.stack(scalars).astype(jnp.int32)
    item_row = item_ids.reshape(1, -1)
    neg_row = neg_ids.reshape(1, -1)
    packed = pack(neg_row, table)
    half = nrows // 2
    odd = (lax.axis_index("shard") & 1) == 1
    piece = jnp.where(odd, packed[half:], jnp.concatenate([packed[:half], packed[2 * half :]], 0))
    other_ids = swap(item_row, "group", 1, groups)
    small = small_rows(item_ids, buckets, lengths, neg_ids)
    bias, allowed, valid, items, partial, panel, spots, zeros = prepare(
        small, lengths.size, rab, where, other_ids, packed, neg_ids.size
    )
    plan, panels, after = [], [], zeros
    for step in sorted(range(1, chips), key=lambda step: -step.bit_count()):
        if step.bit_count() > 1:
            near = swap(piece, "group", 2 * step, groups)
            near = near + zeros
            after = near
            plan += [(step, 1), (step, 2)]
            panels += [near, swap(near, "shard", 1, shards)]
        else:
            plan.append((step, 0))
            panels.append(swap(packed, "group", 2 * step, groups))
    *weights, none = weight_halves(w_in, w_out, after)
    spots = spots + none
    other = fetch(1, plan, spots, items, partial, panel, panels)
    mine = fetch(0, plan, spots, items, partial, panel, panels)
    theirs = swap(other, "group", 1, groups)
    loss, *grads = layer(
        theirs,
        other,
        mine,
        weights=weights,
        b_in=b_in,
        bias=bias,
        allowed=allowed,
        valid=valid,
        ids=small[:1],
        spots=spots,
        parts=shards,
    )
    blocks = [grads[0]] + [swap(grads[step], "shard", step, shards) for step in range(1, shards)]
    blocks = [blocks[0], blocks[-1], *blocks[1:-1]]
    other = gather(chips, spots, blocks, nrows, chips)
    own = gather(0, spots, blocks, nrows, chips) + swap(other, "group", 1, groups)
    total = own[0]
    for step in range(chips - 1, 0, -1):
        total = total + swap(own[step], "group", 2 * step, groups)
    columns = [total] + [swap(total, "shard", step, shards) for step in range(1, shards)]
    plane_row = spots[-1:]
    wide = []
    for spot in range(shards):
        block = columns[0]
        for step in (*range(1, shards, 2), *range(2, shards, 2)):
            block = jnp.where((plane_row ^ step) == spot, columns[step], block)
        wide.append(block)
    return jnp.concatenate(wide, 1), loss


def picker_of(wanted, rows_dev):
    flat = wanted.reshape(-1)
    return (flat[:, None] == jnp.arange(rows_dev, dtype=jnp.int32)[None, :]).astype(F32)


def by_request(item_ids, lengths, buckets, neg_ids, table, w_in, b_in, w_out, rab):
    high = lax.Precision.HIGHEST
    small = small_rows(item_ids, buckets, lengths, neg_ids)
    *weights, _ = weight_halves(w_in, w_out, small)
    bias, allowed, valid = prepare(small, lengths.size, rab)
    groups = lax.axis_size("group")
    rows_dev, width = table.shape
    count = item_ids.shape[0]
    capacity = max(2, 2 * count // groups)
    slots = groups * capacity
    owner = item_ids // rows_dev
    member = (owner[:, None] == jnp.arange(groups, dtype=jnp.int32)[None, :]).astype(jnp.int32)
    rank = jnp.sum(member * (jnp.cumsum(member, 0) - 1), 1)
    target_slot = owner * capacity + rank
    requests = (
        jnp.full((slots,), -1, jnp.int32)
        .at[target_slot]
        .set(item_ids % rows_dev)
        .reshape(groups, capacity)
    )
    own_negatives, _ = unit_of(table[neg_ids.reshape(-1) % rows_dev])
    panel_rows = lax.all_gather(own_negatives, "group", axis=0, tiled=True)
    incoming = lax.all_to_all(requests, "group", split_axis=0, concat_axis=0, tiled=True)
    picker = picker_of(incoming, rows_dev)
    served = jnp.dot(picker, table, precision=high).reshape(groups, capacity, width)
    returned = lax.all_to_all(served, "group", split_axis=0, concat_axis=0, tiled=True)
    emb = returned.reshape(slots, width)[target_slot]
    packed = jnp.concatenate([emb, panel_rows], 0)
    loss, d_emb = layer(
        packed,
        weights=weights,
        b_in=b_in,
        bias=bias,
        allowed=allowed,
        valid=valid,
        ids=small[:1],
        spots=jnp.zeros((1, LANES), jnp.int32),
        parts=1,
    )
    outgoing = jnp.zeros((slots, width), F32).at[target_slot].set(d_emb)
    arrived = lax.all_to_all(
        outgoing.reshape(groups, capacity, width), "group", split_axis=0, concat_axis=0, tiled=True
    )
    partial_grad = jnp.dot(picker.T, arrived.reshape(slots, width), precision=high)
    return lax.psum(partial_grad, "shard"), loss


def body(item_ids, seq_lengths, time_buckets, neg_ids, table, w_in, b_in, w_out, rab):
    groups = lax.axis_size("group")
    shards = lax.axis_size("shard")
    width = table.shape[1]
    small = groups in (2, 4, 8, 16) and shards & (shards - 1) == 0 and shards > 1
    small = small and item_ids.shape[0] == LANES and shards * LANES == width
    plan = direct if small else by_request
    grad, loss = plan(
        item_ids, seq_lengths, time_buckets, neg_ids, table, w_in, b_in, w_out, rab
    )
    return grad, loss.reshape(-1)


def solution(mesh):
    in_specs = (
        P(("shard", "group")),
        P(("shard", "group"), None),
        P(("shard", "group")),
        P("shard", "group"),
        P("group", None),
        P(),
        P(),
        P(),
        P(),
    )
    out_specs = (P("group", None), P(("shard", "group")))
    return jax.shard_map(body, mesh=mesh, in_specs=in_specs, out_specs=out_specs, check_vma=False)
```

```python
import functools

import jax
import jax.numpy as jnp
from jax import lax
from jax.experimental import pallas as pl
from jax.experimental.pallas import tpu as pltpu
from jax.sharding import PartitionSpec as P

MOST_LEN = 64
TEMPER = 0.05
LANES = 128
SUBLANES = 8
F32 = jnp.float32
BF16 = jnp.bfloat16
NN = (((1,), (0,)), ((), ()))
NT = (((1,), (1,)), ((), ()))
TN = (((0,), (0,)), ((), ()))
VMEM = pl.BlockSpec(memory_space=pltpu.VMEM)
SMEM = pl.BlockSpec(memory_space=pltpu.SMEM)


def limit(mebibytes):
    return pltpu.CompilerParams(vmem_limit_bytes=mebibytes * 1024 * 1024)


def halves(value):
    high = value.astype(BF16)
    return high, (value - high.astype(F32)).astype(BF16)


def mul(left, right, dims=NN):
    lh, ll = left
    rh, rl = right
    dot = functools.partial(lax.dot_general, dimension_numbers=dims, preferred_element_type=F32)
    both = dot(jnp.concatenate([lh, ll], 0), rh)
    count = lh.shape[0]
    return both[:count] + (both[count:] + dot(lh, rl))


def mul_small(left, right, dims=NN):
    lh, ll = left
    rh, rl = right
    if dims == NN:
        wide = jnp.concatenate([rh, rl], 1)
        right = jnp.concatenate([wide, wide], 0)
    else:
        right = jnp.concatenate([jnp.concatenate([rh, rh], 1), jnp.concatenate([rl, rl], 1)], 0)
    both = lax.dot_general(jnp.concatenate([lh, ll], 1), right, dims, preferred_element_type=F32)
    half = both.shape[1] // 2
    return both[:, :half] + both[:, half:]


def sum_last(value):
    return jnp.sum(value, axis=-1, keepdims=True)


def mean_last(value):
    return jnp.mean(value, axis=-1, keepdims=True)


def lanes(shape):
    return lax.broadcasted_iota(jnp.int32, shape, 1)


def rows(shape):
    return lax.broadcasted_iota(jnp.int32, shape, 0)


def spread(row, count):
    wide = jnp.broadcast_to(row.astype(F32), (count, count))
    return wide.T.astype(jnp.int32)


def column(row):
    short = LANES - row.shape[1]
    if short:
        row = jnp.concatenate([row, jnp.full((1, short), -1, jnp.int32)], 1)
    return spread(row, LANES)


def norm_of(value):
    centered = value - mean_last(value)
    scale = lax.rsqrt(mean_last(centered * centered) + 1e-05)
    return centered * scale, scale


def norm_back(grad, normed, scale):
    return scale * (grad - mean_last(grad) - normed * mean_last(grad * normed))


def unit_of(value):
    scale = lax.rsqrt(sum_last(value * value) + 1e-06)
    return value * scale, scale


def unit_back(grad, united, scale):
    return scale * (grad - united * sum_last(grad * united))


def time_bias(rab, buckets, bias):
    count = buckets.shape[1]
    gap = jnp.abs(buckets - spread(buckets, count))
    heads, nbuck = rab.shape
    for head in range(heads):
        level = jnp.concatenate([rab[head : head + 1, :], jnp.zeros((1, LANES - nbuck), F32)], 1)
        level = jnp.broadcast_to(level, (count, LANES))
        bias[head] = jnp.take_along_axis(level, gap, axis=1)


def masks(lengths, number):
    square = (LANES, LANES)
    place_i, place_j = rows(square), lanes(square)
    upto = jnp.where(place_i <= place_j, spread(lengths, LANES), 0)
    ends = spread(jnp.sum(upto, axis=0, keepdims=True), LANES)
    real = place_i < number
    seg = jnp.sum((real & (place_j >= ends)).astype(jnp.int32), axis=0, keepdims=True)
    following = jnp.sum((real & (place_j + 1 >= ends)).astype(jnp.int32), axis=0, keepdims=True)
    near = (seg == following) & (lanes((1, LANES)) + 1 < LANES)
    allowed = (place_j <= place_i) & (spread(seg, LANES) == seg)
    valid = spread(near.astype(jnp.int32), LANES)
    return jnp.where(allowed, 1.0 / MOST_LEN, 0.0).astype(F32), valid.astype(F32)


def weights_kernel(w_in, w_out, after, in_h, in_l, in_th, in_tl, out_h, out_l, out_th, out_tl, zeros):
    width, hidden = w_in.shape
    zeros[...] = jnp.zeros(zeros.shape, jnp.int32)
    high, low = halves(w_out[...])
    out_h[...], out_l[...] = high, low
    out_th[...], out_tl[...] = high.T, low.T
    for start in range(0, hidden, width):
        span = slice(start, start + width)
        high, low = halves(w_in[:, span])
        in_h[:, span], in_l[:, span] = high, low
        in_th[span, :], in_tl[span, :] = high.T, low.T


def weight_halves(w_in, w_out, after):
    width, hidden = w_in.shape
    shapes = [(width, hidden)] * 2 + [(hidden, width)] * 2 + [(width, width)] * 4
    return pl.pallas_call(
        weights_kernel,
        out_shape=(
            *(jax.ShapeDtypeStruct(shape, BF16) for shape in shapes),
            jax.ShapeDtypeStruct((1, LANES), jnp.int32),
        ),
        in_specs=[VMEM] * 2 + [pl.BlockSpec(memory_space=pl.ANY)],
        out_specs=(VMEM,) * 9,
        compiler_params=limit(8),
        cost_estimate=pl.CostEstimate(flops=4_000_000, bytes_accessed=15_000_000, transcendentals=0),
        name="weight_halves",
    )(w_in, w_out, after)


def prepare_kernel(number, small, rab, bias, allowed, valid):
    allowed[...], valid[...] = masks(small[2:3], number)
    time_bias(rab, small[1:2], bias)


def prepare_own_kernel(number, nneg, where, small, rab, other_ids, shard, *outs):
    *pairs, items, found, panel, spots, zeros = outs
    zeros[...] = jnp.zeros(zeros.shape, F32)
    for index in range(where.shape[0]):
        spots[index : index + 1, :] = jnp.full((1, LANES), where[index], jnp.int32)
    prepare_kernel(number, small, rab, *pairs)
    count = other_ids.shape[1]
    me, other = spread(small[0:1], count), spread(other_ids[...], count)
    items[:count] = me
    items[count:] = other
    names = jnp.concatenate([me, other, spread(small[3:4], LANES)[:nneg]], 0)
    chosen = chosen_rows(names, [(where[0], None, shard[...])])
    found[...] = chosen[: 2 * count]
    panel[...] = unit_of(chosen[2 * count :])[0]


def small_rows(*values):
    total = 0
    for row, value in enumerate(values):
        spots = [(row, len(values) - 1 - row, 0), (0, LANES - value.size, 0)]
        total = total + lax.pad(value.reshape(1, -1), jnp.int32(0), spots)
    return total


def prepare(small, number, rab, where=None, other_ids=None, shard=None, nneg=0):
    count = small.shape[1]
    heads = rab.shape[0]
    sds = jax.ShapeDtypeStruct
    outs = (sds((heads, count, count), F32), *(sds((count, count), F32),) * 2)
    kernel, args, specs = functools.partial(prepare_kernel, number), (small, rab), []
    if where is not None:
        kernel, specs = functools.partial(prepare_own_kernel, number, nneg), [SMEM]
        args = (where, *args, other_ids, shard)
        width = shard.shape[1]
        outs += (
            sds((2 * count, count), jnp.int32),
            sds((2 * count, width), F32),
            sds((nneg, width), F32),
            sds((where.shape[0], LANES), jnp.int32),
            sds((1, width), F32),
        )
    return pl.pallas_call(
        kernel,
        out_shape=outs,
        in_specs=specs + [VMEM] * (len(args) - len(specs)),
        out_specs=(VMEM,) * len(outs),
        compiler_params=limit(6),
        cost_estimate=pl.CostEstimate(flops=200_000_000, bytes_accessed=2_000_000, transcendentals=0),
        name="prepare",
    )(*args)


def layer_kernel(pieces, spots, *refs):
    packed = refs[:pieces]
    in_h, in_l, in_th, in_tl, out_h, out_l, out_th, out_tl = refs[pieces : pieces + 8]
    b_in, bias, allowed_ref, valid_ref, ids = refs[pieces + 8 : pieces + 13]
    loss_ref = refs[pieces + 13]
    grads = refs[pieces + 14 :]
    heads, count, _ = bias.shape
    width = in_h.shape[0]
    each = width // heads
    emb = packed[0][:count]
    if pieces > 1:
        emb = emb + packed[2][...]
    allowed = allowed_ref[...]
    valid = valid_ref[:, :1]
    square = (count, count)
    place_i, place_j = rows(square), lanes(square)
    xn, x_scale = norm_of(emb)
    w_out = (out_h[...], out_l[...])
    xn_parts = halves(xn)
    hidden, slope = {}, {}

    def project(start, size):
        span = slice(start, start + size)
        pre = mul(xn_parts, (in_h[:, span], in_l[:, span])) + b_in[:, span]
        sig = jax.nn.sigmoid(pre)
        return pre * sig, sig * (1.0 + pre * (1.0 - sig))

    for part in (2, 3, 1):
        hidden[part], slope[part] = project(width * part, width)
    gates = []
    kept = []
    mixed = []
    for head in range(heads):
        if head % 2 == 0:
            gates.append(project(each * head, 2 * each))
        vh, qh, kh = (
            halves(hidden[part][:, each * head : each * (head + 1)])
            for part in (1, 2, 3)
        )
        score = mul_small(qh, kh, NT) * each ** (-0.5) + bias[head]
        gate = jax.nn.sigmoid(score)
        weight = score * gate * allowed
        bend = gate * (1.0 + score * (1.0 - gate)) * allowed
        mixed.append(mul_small(halves(weight), vh))
        kept.append((vh, qh, kh, halves(weight.T), bend))
    upart, slope[0] = (jnp.concatenate(pair, axis=1) for pair in zip(*gates))
    yn, y_scale = norm_of(jnp.concatenate(mixed, axis=1))
    out = mul(halves(yn * upart), w_out) + emb
    states, s_scale = unit_of(out)
    united, e_scale = unit_of(emb)
    last = rows((count, width)) == count - 1
    target = jnp.where(last, 0.0, pltpu.roll(united, count - 1, 0))
    positive = sum_last(states * target) * (1.0 / TEMPER)
    expos = jnp.exp(positive)
    state_parts = halves(states)
    panel = halves(jnp.concatenate([piece[count:] for piece in packed[:2]], 0))
    logits = mul(state_parts, panel, NT) * (1.0 / TEMPER)
    exps = jnp.exp(logits)
    zneg = sum_last(exps)
    tilt = sum_last(exps * logits)
    pulled = mul(halves(exps), panel)
    total = expos + zneg
    loss = valid * (jnp.log(total) - positive)
    loss_ref[...] = jnp.sum(jnp.where(place_i == place_j, loss, 0.0), axis=0, keepdims=True)
    share = valid * (expos / total - 1.0) * (1.0 / TEMPER)
    d_states = share * target + pulled * (valid / total * (1.0 / TEMPER))
    d_out = s_scale * (d_states - states * (share * TEMPER * positive + tilt * (valid / total)))
    first = rows((count, width)) == 0
    d_next = jnp.where(first, 0.0, pltpu.roll(share * states, 1, 0))
    d_emb = d_out + unit_back(d_next, united, e_scale)
    d_gated = mul(halves(d_out), (out_th[...], out_tl[...]))
    d_mixed = norm_back(d_gated * upart, yn, y_scale)

    def input_grad(part, start, grad):
        span = slice(width * part + start, width * part + start + 2 * each)
        return mul(halves(grad * slope[part][:, start : start + 2 * each]), (in_th[span], in_tl[span]))

    d_gate = d_gated * yn
    d_xn = jnp.zeros((count, width), F32)
    for start in range(0, width, 2 * each):
        d_xn = d_xn + input_grad(0, start, d_gate[:, start : start + 2 * each])
        d_v, d_q, d_k = [], [], []
        for head in (start // each, start // each + 1):
            vh, qh, kh, weight_t, bend = kept[head]
            d_mh = halves(d_mixed[:, each * head : each * (head + 1)])
            d_v.append(mul_small(weight_t, d_mh))
            d_score = mul_small(d_mh, vh, NT) * bend * each ** (-0.5)
            d_q.append(mul_small(halves(d_score), kh))
            d_k.append(mul_small(halves(d_score.T), qh))
        for part, grad in ((1, d_v), (2, d_q), (3, d_k)):
            d_xn = d_xn + input_grad(part, start, jnp.concatenate(grad, axis=1))
    d_emb = d_emb + norm_back(d_xn, xn, x_scale)
    if len(grads) == 1:
        grads[0][...] = d_emb
        return
    part = width // len(grads)
    plane = spots[spots.shape[0] - 1 :, :part]
    for step, out_ref in enumerate(grads):
        block = d_emb[:, :part]
        for spot in range(1, len(grads)):
            mine = (plane ^ step) == spot
            block = jnp.where(mine, d_emb[:, part * spot : part * (spot + 1)], block)
        out_ref[:count] = block
        out_ref[count:] = jnp.broadcast_to(ids[...].astype(F32), (SUBLANES, part))


def layer(*packed, weights, b_in, bias, allowed, valid, ids, spots, parts):
    heads, count, _ = bias.shape
    extra = SUBLANES if parts > 1 else 0
    width = weights[0].shape[0]
    sds = jax.ShapeDtypeStruct
    return pl.pallas_call(
        functools.partial(layer_kernel, len(packed)),
        out_shape=(sds((1, count), F32),) + (sds((count + extra, width // parts), F32),) * parts,
        in_specs=[VMEM] * (len(packed) + 14),
        out_specs=(VMEM,) * (1 + parts),
        compiler_params=limit(14 if parts > 1 else 40),
        cost_estimate=pl.CostEstimate(
            flops=2_500_000_000, bytes_accessed=8_000_000, transcendentals=400_000
        ),
        name="layer",
    )(spots, *packed, *weights, b_in.reshape(1, -1), bias, allowed, valid, ids)


def pack(neg_ids, table):
    nrows, width = table.shape
    body = lax.pad(table, jnp.float32(0), [(0, SUBLANES, 0), (0, 0, 0)])
    tile = [(nrows, SUBLANES - 1, 0), (0, width - neg_ids.shape[1], 0)]
    return body + lax.pad(neg_ids, jnp.int32(0), tile).astype(F32)


def chosen_rows(names, pieces):
    place = jnp.full(names.shape, -1, jnp.int32)
    offset = 0
    for owner, part, held in pieces:
        nrows = held.shape[0] - SUBLANES
        if part is None:
            spot = names - owner * nrows
        else:
            spot = names - (owner * 2 + part) * nrows
        place = jnp.where((spot >= 0) & (spot < nrows), spot + offset, place)
        offset += held.shape[0]
    rest = -offset % LANES
    held = [piece[2] for piece in pieces]
    if rest:
        held.append(jnp.zeros((rest, held[0].shape[1]), F32))
    column = lanes(names.shape)
    hot = [place == column + start for start in range(0, offset + rest, LANES)]
    hot = jnp.where(jnp.concatenate(hot, 1), 1.0, 0.0).astype(BF16)
    high, low = halves(jnp.concatenate(held, 0))
    dot = functools.partial(lax.dot_general, dimension_numbers=NN, preferred_element_type=F32)
    return dot(hot, high) + dot(hot, low)


def fetch_kernel(side, plan, spots, items, partial, panel, *refs):
    *shards, out_ref = refs
    nneg = panel.shape[0]
    count = items.shape[1]
    odd = spots[spots.shape[0] - 1 :, :] & 1
    pieces, wanted = [], []
    for (step, kind), shard in zip(plan, shards):
        nrows = shard.shape[0] - SUBLANES
        part = {0: None, 1: odd, 2: 1 - odd}[kind]
        pieces.append((spots[step : step + 1], part, shard[...]))
        if kind < 2:
            wanted.append(shard[nrows : nrows + 1, :nneg].astype(jnp.int32))
    far = nneg * len(wanted)
    names = items[count * side : count * (side + 1)]
    if side:
        names = jnp.concatenate([names, column(jnp.concatenate(wanted, 1))[:far]], 0)
    chosen = chosen_rows(names, pieces)
    out_ref[:count] = partial[count * side : count * (side + 1)] + chosen[:count]
    if side:
        out_ref[count : count + nneg] = panel[...]
        out_ref[count + nneg :] = unit_of(chosen[count:])[0]


def fetch(side, plan, spots, items, partial, panel, shards):
    nneg, width = panel.shape
    count = items.shape[1]
    owners = 1 + len({step for step, _ in plan})
    extra = nneg * owners if side else 0
    return pl.pallas_call(
        functools.partial(fetch_kernel, side, plan),
        out_shape=jax.ShapeDtypeStruct((count + extra, width), F32),
        in_specs=[VMEM] * (4 + len(shards)),
        out_specs=VMEM,
        compiler_params=limit(6),
        cost_estimate=pl.CostEstimate(flops=200_000_000, bytes_accessed=2_000_000, transcendentals=0),
        name="fetch",
    )(spots, items, partial, panel, *shards)


def gather_kernel(first, spots, *refs):
    *grads, out_ref = refs
    count = grads[0].shape[0] - SUBLANES
    tokens = [jnp.concatenate(halves(grad[:count]), 1) for grad in grads]
    tokens = jnp.concatenate(tokens, 0)
    names = jnp.concatenate([grad[count : count + 1] for grad in grads], 1).astype(jnp.int32)
    chips, nrows, part = out_ref.shape
    for step in range(chips):
        base = jnp.concatenate([spots[first + step : first + step + 1, :count] * nrows] * len(grads), 1)
        hot = rows((nrows, names.shape[1])) == names - base
        hot = jnp.where(hot, 1.0, 0.0).astype(BF16)
        both = lax.dot_general(hot, tokens, NN, preferred_element_type=F32)
        out_ref[step] = both[:, :part] + both[:, part:]


def gather(first, spots, grads, nrows, chips):
    return pl.pallas_call(
        functools.partial(gather_kernel, first),
        out_shape=jax.ShapeDtypeStruct((chips, nrows, grads[0].shape[1]), F32),
        in_specs=[VMEM] * (1 + len(grads)),
        out_specs=VMEM,
        compiler_params=limit(4),
        cost_estimate=pl.CostEstimate(flops=150_000_000, bytes_accessed=1_000_000, transcendentals=0),
        name="gather",
    )(spots, *grads)


def swap(value, axis, step, size):
    return lax.ppermute(value, axis, [(i, i ^ step) for i in range(size)])


def direct(item_ids, lengths, buckets, neg_ids, table, w_in, b_in, w_out, rab):
    groups = lax.axis_size("group")
    shards = lax.axis_size("shard")
    group = lax.axis_index("group")
    chips = groups // 2
    nrows = table.shape[0]
    own_side = [group ^ (2 * step) for step in range(chips)]
    scalars = own_side + [index ^ 1 for index in own_side] + [lax.axis_index("shard")]
    where = jnp.stack(scalars).astype(jnp.int32)
    item_row = item_ids.reshape(1, -1)
    neg_row = neg_ids.reshape(1, -1)
    packed = pack(neg_row, table)
    half = nrows // 2
    odd = (lax.axis_index("shard") & 1) == 1
    piece = jnp.where(odd, packed[half:], jnp.concatenate([packed[:half], packed[2 * half :]], 0))
    other_ids = swap(item_row, "group", 1, groups)
    small = small_rows(item_ids, buckets, lengths, neg_ids)
    bias, allowed, valid, items, partial, panel, spots, zeros = prepare(
        small, lengths.size, rab, where, other_ids, packed, neg_ids.size
    )
    plan, panels, after = [], [], zeros
    for step in sorted(range(1, chips), key=lambda step: -step.bit_count()):
        if step.bit_count() > 1:
            near = swap(piece, "group", 2 * step, groups)
            near = near + zeros
            after = near
            plan += [(step, 1), (step, 2)]
            panels += [near, swap(near, "shard", 1, shards)]
        else:
            plan.append((step, 0))
            panels.append(swap(packed, "group", 2 * step, groups))
    *weights, none = weight_halves(w_in, w_out, after)
    spots = spots + none
    other = fetch(1, plan, spots, items, partial, panel, panels)
    mine = fetch(0, plan, spots, items, partial, panel, panels)
    theirs = swap(other, "group", 1, groups)
    loss, *grads = layer(
        theirs,
        other,
        mine,
        weights=weights,
        b_in=b_in,
        bias=bias,
        allowed=allowed,
        valid=valid,
        ids=small[:1],
        spots=spots,
        parts=shards,
    )
    blocks = [grads[0]] + [swap(grads[step], "shard", step, shards) for step in range(1, shards)]
    blocks = [blocks[0], blocks[-1], *blocks[1:-1]]
    half = chips // 2
    sums = {}
    for first in (half, 0):
        other = gather(chips + first, spots, blocks, nrows, half)
        pair = gather(first, spots, blocks, nrows, half) + swap(other, "group", 1, groups)
        sums.update({first + index: pair[index] for index in range(half)})
    total = sums[0]
    for step in range(chips - 1, 0, -1):
        total = total + swap(sums[step], "group", 2 * step, groups)
    columns = [total] + [swap(total, "shard", step, shards) for step in range(1, shards)]
    plane_row = spots[-1:]
    wide = []
    for spot in range(shards):
        block = columns[0]
        for step in (*range(1, shards, 2), *range(2, shards, 2)):
            block = jnp.where((plane_row ^ step) == spot, columns[step], block)
        wide.append(block)
    return jnp.concatenate(wide, 1), loss


def picker_of(wanted, rows_dev):
    flat = wanted.reshape(-1)
    return (flat[:, None] == jnp.arange(rows_dev, dtype=jnp.int32)[None, :]).astype(F32)


def by_request(item_ids, lengths, buckets, neg_ids, table, w_in, b_in, w_out, rab):
    high = lax.Precision.HIGHEST
    small = small_rows(item_ids, buckets, lengths, neg_ids)
    *weights, _ = weight_halves(w_in, w_out, small)
    bias, allowed, valid = prepare(small, lengths.size, rab)
    groups = lax.axis_size("group")
    rows_dev, width = table.shape
    count = item_ids.shape[0]
    capacity = max(2, 2 * count // groups)
    slots = groups * capacity
    owner = item_ids // rows_dev
    member = (owner[:, None] == jnp.arange(groups, dtype=jnp.int32)[None, :]).astype(jnp.int32)
    rank = jnp.sum(member * (jnp.cumsum(member, 0) - 1), 1)
    target_slot = owner * capacity + rank
    requests = (
        jnp.full((slots,), -1, jnp.int32)
        .at[target_slot]
        .set(item_ids % rows_dev)
        .reshape(groups, capacity)
    )
    own_negatives, _ = unit_of(table[neg_ids.reshape(-1) % rows_dev])
    panel_rows = lax.all_gather(own_negatives, "group", axis=0, tiled=True)
    incoming = lax.all_to_all(requests, "group", split_axis=0, concat_axis=0, tiled=True)
    picker = picker_of(incoming, rows_dev)
    served = jnp.dot(picker, table, precision=high).reshape(groups, capacity, width)
    returned = lax.all_to_all(served, "group", split_axis=0, concat_axis=0, tiled=True)
    emb = returned.reshape(slots, width)[target_slot]
    packed = jnp.concatenate([emb, panel_rows], 0)
    loss, d_emb = layer(
        packed,
        weights=weights,
        b_in=b_in,
        bias=bias,
        allowed=allowed,
        valid=valid,
        ids=small[:1],
        spots=jnp.zeros((1, LANES), jnp.int32),
        parts=1,
    )
    outgoing = jnp.zeros((slots, width), F32).at[target_slot].set(d_emb)
    arrived = lax.all_to_all(
        outgoing.reshape(groups, capacity, width), "group", split_axis=0, concat_axis=0, tiled=True
    )
    partial_grad = jnp.dot(picker.T, arrived.reshape(slots, width), precision=high)
    return lax.psum(partial_grad, "shard"), loss


def body(item_ids, seq_lengths, time_buckets, neg_ids, table, w_in, b_in, w_out, rab):
    groups = lax.axis_size("group")
    shards = lax.axis_size("shard")
    width = table.shape[1]
    small = groups in (2, 4, 8, 16) and shards & (shards - 1) == 0 and shards > 1
    small = small and item_ids.shape[0] == LANES and shards * LANES == width
    plan = direct if small else by_request
    grad, loss = plan(
        item_ids, seq_lengths, time_buckets, neg_ids, table, w_in, b_in, w_out, rab
    )
    return grad, loss.reshape(-1)


def solution(mesh):
    in_specs = (
        P(("shard", "group")),
        P(("shard", "group"), None),
        P(("shard", "group")),
        P("shard", "group"),
        P("group", None),
        P(),
        P(),
        P(),
        P(),
    )
    out_specs = (P("group", None), P(("shard", "group")))
    return jax.shard_map(body, mesh=mesh, in_specs=in_specs, out_specs=out_specs, check_vma=False)
```
